32 devices in a mesh: seq: 16 (over z, y, core), tensor: 2 (over x).
Axes of the slice: x: 2, y: 2, z: 4, core: 2. Of those that a mesh axis runs over, the one named last changes fastest.
Arguments:
- hidden_in: bfloat16 [4096, 8192], P('seq', 'tensor'), may hold values from -6 to 6
- frozen_query: bfloat16 [4096, 8192], P('seq', 'tensor'), may hold values from -48 to 48
- key_base: bfloat16 [4096, 1024], P('seq', 'tensor'), may hold values from -6 to 6
- frozen_value: bfloat16 [4096, 1024], P('seq', 'tensor'), may hold values from -6 to 6
- down_query: bfloat16 [8192, 16], P('tensor'), may hold values from -0.0625 to 0.0625
- query_upper_factor: bfloat16 [16, 8192], P(None, 'tensor'), may hold values from -1.5 to 1.5
- down_value: bfloat16 [8192, 16], P('tensor'), may hold values from -0.0625 to 0.0625
- value_upper_factor: bfloat16 [16, 1024], P(None, 'tensor'), may hold values from -1.5 to 1.5
- grad_output: bfloat16 [4096, 8192], P('seq', 'tensor'), may hold values from -6 to 6
Outputs:
- attention: bfloat16 [4096, 8192], P('seq', 'tensor')
- grad_down_query: float32 [8192, 16], P('tensor')
- gradient_query_upper: float32 [16, 8192], P(None, 'tensor')
- grad_down_value: float32 [8192, 16], P('tensor')
- gradient_value_upper: float32 [16, 1024], P(None, 'tensor')
The draws below stay inside these ranges and needn't reach their ends.
All inputs are finite; a program needn't handle non-finite values.
Results may differ from the reference program's by a relative error of at most 0.024.
Values may be sent and summed in bfloat16 or wider, within the bound.
No kernel may reach another device: no remote copies, remote signals or barrier semaphores. Data moves between devices by JAX's collectives and lax.ppermute only.
A program may use at most 192 MiB of HBM per device.

```python
import jax
import jax.numpy as jnp
from jax import lax

D = 8192
H = 64
KV = 8
HD = 128
R = 16
GROUP = 2048
TOKENS = 4096


def draw_key_base(key, part):
    base_key = jax.random.fold_in(key, 7)
    result = jnp.clip(jax.random.normal(jax.random.fold_in(base_key, 2), (TOKENS, KV, HD)), -6.0, 6.0)
    return result.reshape(TOKENS, KV * HD).astype(jnp.bfloat16)


def draw_frozen_query(key, part):
    base_key = jax.random.fold_in(key, 7)
    result = jnp.clip(jax.random.normal(jax.random.fold_in(base_key, 5), (TOKENS, H, HD)), -6.0, 6.0)
    return result.reshape(TOKENS, H * HD).astype(jnp.bfloat16)


def level_of(stream_key, extent, shards, least, high):
    level = 1.0
    for axis_at, blocks in shards:
        draws = jax.random.uniform(jax.random.fold_in(jax.random.fold_in(stream_key, 6), axis_at), (blocks,), jnp.float32, least / len(shards), high / len(shards))
        level = level * jnp.repeat(jnp.exp(draws), extent[axis_at] // blocks).reshape((-1,) + (1,) * (len(extent) - 1 - axis_at))
    return level


def gaussian(rng, extent, width, limit, cuts=(), kind=jnp.bfloat16):
    factor_of = level_of(rng, extent, cuts, -0.22, 0.18) if cuts else 1.0
    values = jax.random.normal(rng, extent, jnp.float32) * width * factor_of
    return jnp.minimum(jnp.maximum(values, -limit), limit).astype(kind)


def setup_inputs(seed: int = 0) -> dict:
    seeds = jax.random.split(jax.random.key(seed), 10)
    hidden_in = gaussian(seeds[0], (TOKENS, D), 1.0, 6.0, ((0, 16), (1, 2)))
    frozen_query = draw_frozen_query(jax.random.fold_in(seeds[9], 71), 0)
    key_base = draw_key_base(jax.random.fold_in(seeds[9], 71), 0)
    frozen_value = gaussian(seeds[3], (TOKENS, KV * HD), 1.0, 6.0, ((0, 16), (1, 2)))
    down_query = gaussian(seeds[4], (D, R), D ** -0.5, 0.0625, ((0, 2),))
    query_upper_factor = gaussian(seeds[5], (R, H * HD), R ** -0.5, 1.5, ((1, 2),))
    down_value = gaussian(seeds[6], (D, R), D ** -0.5, 0.0625, ((0, 2),))
    value_upper_factor = gaussian(seeds[7], (R, KV * HD), R ** -0.5, 1.5, ((1, 2),))
    grad_output = gaussian(seeds[8], (TOKENS, H * HD), 1.0, 6.0, ((0, 16), (1, 2)))
    return {"hidden_in": hidden_in, "frozen_query": frozen_query, "key_base": key_base, "frozen_value": frozen_value, "down_query": down_query, "query_upper_factor": query_upper_factor, "down_value": down_value, "value_upper_factor": value_upper_factor, "grad_output": grad_output}


ADAPTER_SCALE = 0.5


def attend_group(inputs):
    query_matrix, keys, value_matrix, upstream = inputs
    scale_inv = float(HD) ** -0.5
    length = keys.shape[0]
    scores = jnp.einsum('tpd,sd->pts', query_matrix.astype(jnp.float32), keys.astype(jnp.float32)) * scale_inv
    causal = jnp.arange(length)[:, None] >= jnp.arange(length)[None, :]
    scores = jnp.where(causal, scores, -jnp.inf)
    row_max = jnp.max(scores, axis=-1, keepdims=True)
    lse = row_max + jnp.log(jnp.sum(jnp.exp(scores - row_max), axis=-1, keepdims=True))
    probs = jnp.exp(scores - lse)
    probs_bf = probs.astype(jnp.bfloat16)
    output = jnp.einsum('pts,sd->tpd', probs_bf.astype(jnp.float32), value_matrix.astype(jnp.float32)).astype(jnp.bfloat16)
    row_delta = jnp.sum(upstream.astype(jnp.float32) * output.astype(jnp.float32), axis=-1)
    grad_probs = jnp.einsum('tpd,sd->pts', upstream.astype(jnp.float32), value_matrix.astype(jnp.float32))
    grad_scores = (probs * (grad_probs - jnp.transpose(row_delta)[:, :, None]) * scale_inv).astype(jnp.bfloat16)
    grad_query = jnp.einsum('pts,sd->tpd', grad_scores.astype(jnp.float32), keys.astype(jnp.float32)).astype(jnp.bfloat16)
    grad_value = jnp.einsum('pts,tpd->sd', probs_bf.astype(jnp.float32), upstream.astype(jnp.float32)).astype(jnp.bfloat16)
    return output, grad_query, grad_value


def attend_head(inputs):
    head_index, query_matrix, keys, value_matrix, upstream = inputs
    per_head = H // KV
    shift_rows = jnp.where(head_index >= KV // 2, GROUP // 2, 0).astype(jnp.int32)
    groups = TOKENS // GROUP
    rolled_q = jnp.roll(query_matrix, -shift_rows, axis=0).reshape(groups, GROUP, per_head, HD)
    rolled_k = jnp.roll(keys, -shift_rows, axis=0).reshape(groups, GROUP, HD)
    rolled_v = jnp.roll(value_matrix, -shift_rows, axis=0).reshape(groups, GROUP, HD)
    rolled_g = jnp.roll(upstream, -shift_rows, axis=0).reshape(groups, GROUP, per_head, HD)
    output, grad_query, grad_value = lax.map(attend_group, (rolled_q, rolled_k, rolled_v, rolled_g))
    output = jnp.roll(output.reshape(TOKENS, per_head, HD), shift_rows, axis=0)
    grad_query = jnp.roll(grad_query.reshape(TOKENS, per_head, HD), shift_rows, axis=0)
    grad_value = jnp.roll(grad_value.reshape(TOKENS, HD), shift_rows, axis=0)
    return output, grad_query, grad_value


def reference(hidden_in, frozen_query, key_base, frozen_value, down_query, query_upper_factor, down_value, value_upper_factor, grad_output):
    per_head = H // KV
    reduced_query = jnp.dot(hidden_in, down_query, preferred_element_type=jnp.float32).astype(jnp.bfloat16)
    reduced_value = jnp.dot(hidden_in, down_value, preferred_element_type=jnp.float32).astype(jnp.bfloat16)
    query_matrix = (frozen_query.astype(jnp.float32) + ADAPTER_SCALE * jnp.dot(reduced_query, query_upper_factor, preferred_element_type=jnp.float32)).astype(jnp.bfloat16)
    value_matrix = (frozen_value.astype(jnp.float32) + ADAPTER_SCALE * jnp.dot(reduced_value, value_upper_factor, preferred_element_type=jnp.float32)).astype(jnp.bfloat16)
    head_q = jnp.transpose(query_matrix.reshape(TOKENS, KV, per_head, HD), (1, 0, 2, 3))
    head_k = jnp.transpose(key_base.reshape(TOKENS, KV, HD), (1, 0, 2))
    head_v = jnp.transpose(value_matrix.reshape(TOKENS, KV, HD), (1, 0, 2))
    head_g = jnp.transpose(grad_output.reshape(TOKENS, KV, per_head, HD), (1, 0, 2, 3))
    head_index = jnp.arange(KV, dtype=jnp.int32)
    output, grad_query, grad_value = lax.map(attend_head, (head_index, head_q, head_k, head_v, head_g))
    attention = jnp.transpose(output, (1, 0, 2, 3)).reshape(TOKENS, H * HD)
    query_gradient_rows = jnp.transpose(grad_query, (1, 0, 2, 3)).reshape(TOKENS, H * HD)
    value_gradient_rows = jnp.transpose(grad_value, (1, 0, 2)).reshape(TOKENS, KV * HD)
    gradient_query_upper = jnp.dot(reduced_query.T, query_gradient_rows, preferred_element_type=jnp.float32) * ADAPTER_SCALE
    gradient_value_upper = jnp.dot(reduced_value.T, value_gradient_rows, preferred_element_type=jnp.float32) * ADAPTER_SCALE
    restored_query = (ADAPTER_SCALE * jnp.dot(query_gradient_rows, query_upper_factor.T, preferred_element_type=jnp.float32)).astype(jnp.bfloat16)
    restored_value = (ADAPTER_SCALE * jnp.dot(value_gradient_rows, value_upper_factor.T, preferred_element_type=jnp.float32)).astype(jnp.bfloat16)
    grad_down_query = jnp.dot(hidden_in.T, restored_query, preferred_element_type=jnp.float32)
    grad_down_value = jnp.dot(hidden_in.T, restored_value, preferred_element_type=jnp.float32)
    return (attention, grad_down_query, gradient_query_upper, grad_down_value, gradient_value_upper)
```

```python
import functools

import jax
import jax.numpy as jnp
from jax import lax
from jax.experimental import pallas as pl
from jax.experimental.pallas import tpu as pltpu
from jax.sharding import PartitionSpec as P

HD = 128
GROUP = 2048
ADAPTER_SCALE = 0.5
LOG2E = 1.4426950408889634
MASKED = -1e30

F32 = jnp.float32
BF16 = jnp.bfloat16
NN = (((1,), (0,)), ((), ()))
NT = (((1,), (1,)), ((), ()))

AXES = ("seq", "tensor")


def dot(a, b, dims):
    return lax.dot_general(a, b, dims, preferred_element_type=F32)


def attention_body(rows, per_head, pieces, where, *refs):
    frozen, low_q, low_q_t, up_q, up_v, low_v, grad_out = refs[:7]
    keys = refs[7 : 7 + pieces]
    values = refs[7 + pieces : 7 + 2 * pieces]
    out, grad_up_q, back_q, back_v, grad_up_v = refs[7 + 2 * pieces : 12 + 2 * pieces]
    scores, probs, wide_v, grad_v = refs[12 + 2 * pieces :]
    scale = float(HD) ** -0.5
    place, y_bit, z_bit = where[0], where[1], where[2]
    for j in range(pieces):
        wide_v[j * rows : (j + 1) * rows, :HD] = values[j][...]
        wide_v[j * rows : (j + 1) * rows, HD:] = jnp.ones((rows, HD), BF16)
    grad_v[...] = jnp.zeros_like(grad_v)

    @pl.when(pl.program_id(0) == 0)
    def _():
        back_q[...] = jnp.zeros_like(back_q)
        back_v[...] = jnp.zeros_like(back_v)

    row_at = lax.broadcasted_iota(jnp.int32, (rows, rows), 0)
    col_at = lax.broadcasted_iota(jnp.int32, (rows, rows), 1)

    def heads_over(blocks):
        def one_head(h, carry):
            cols = pl.ds(pl.multiple_of(h * HD, HD), HD)
            up = up_q[:, cols]
            query = (frozen[:, cols].astype(F32) + ADAPTER_SCALE * dot(low_q[...], up, NN)).astype(BF16)
            top = None
            for j in blocks:
                s = dot(query, keys[j][...], NT) * (scale * LOG2E)
                if j == 0:
                    s = jnp.where(row_at >= col_at, s, MASKED)
                if j == 1:
                    s = jnp.where(place > 0, s, MASKED)
                scores[:, j * rows : (j + 1) * rows] = s
                top = s if top is None else jnp.maximum(top, s)
            row_max = jnp.max(top, axis=1, keepdims=True)
            total = jnp.zeros((rows, 2 * HD), F32)
            for j in blocks:
                e = jnp.exp2(scores[:, j * rows : (j + 1) * rows] - row_max).astype(BF16)
                probs[:, j * rows : (j + 1) * rows] = e
                total = total + dot(e, wide_v[j * rows : (j + 1) * rows, :], NN)
            inverse = 1.0 / total[:, HD:]
            attended = (total[:, :HD] * inverse).astype(BF16)
            out[:, cols] = attended
            upstream = grad_out[:, cols]
            upstream_f = upstream.astype(F32)
            delta = jnp.sum(upstream_f * attended.astype(F32), axis=1, keepdims=True)
            normed_t = (upstream_f * inverse).astype(BF16).T
            grad_query = jnp.zeros((rows, HD), F32)
            for j in blocks:
                grad_probs = dot(upstream, values[j][...], NT)
                e = probs[:, j * rows : (j + 1) * rows]
                grad_s = (e.astype(F32) * (grad_probs - delta)).astype(BF16)
                grad_query = grad_query + dot(grad_s, keys[j][...], NN)
                grad_v[:, j * rows : (j + 1) * rows] += dot(normed_t, e, NN)
            grad_query = (grad_query * (inverse * scale)).astype(BF16)
            grad_up_q[:, cols] = ADAPTER_SCALE * dot(low_q_t[...], grad_query, NN)
            back_q[...] += ADAPTER_SCALE * dot(up, grad_query, NT)
            return carry

        lax.fori_loop(0, per_head, one_head, 0, unroll=2)

    for y in (0, 1):
        for z in (0, 1):

            @pl.when((y_bit == y) & (z_bit == z))
            def _():
                blocks = [0, 1]
                if y:
                    blocks += [2, 3]
                if z:
                    blocks += [4, 5, 6, 7]
                heads_over(blocks)

    rounded = grad_v[...].astype(BF16)
    back_v[...] += ADAPTER_SCALE * dot(up_v[...], rounded, NN)
    grad_up_v[...] = ADAPTER_SCALE * dot(low_v[...], rounded, NT)


def attention_call(where, frozen, low_q, low_q_t, up_q, up_v, low_v, grad_out, keys, values):
    rows, width = frozen.shape
    kv = keys[0].shape[1] // HD
    rank = up_q.shape[0]
    pieces = len(keys)
    wide = width // kv
    per_head = wide // HD

    def columns(height, wide_of):
        return pl.BlockSpec((height, wide_of), lambda g, w: (0, g))

    def whole(shape):
        return pl.BlockSpec(shape, lambda g, w: (0, 0))

    pairs = rows * rows * per_head * kv * pieces
    return pl.pallas_call(
        functools.partial(attention_body, rows, per_head, pieces),
        grid_spec=pltpu.PrefetchScalarGridSpec(
            num_scalar_prefetch=1,
            grid=(kv,),
            in_specs=[
                columns(rows, wide),
                whole((rows, rank)),
                whole((rank, rows)),
                columns(rank, wide),
                columns(rank, HD),
                whole((rank, pieces * rows)),
                columns(rows, wide),
            ]
            + [columns(rows, HD)] * (2 * pieces),
            out_specs=[
                columns(rows, wide),
                columns(rank, wide),
                whole((rank, rows)),
                whole((rank, pieces * rows)),
                columns(rank, HD),
            ],
            scratch_shapes=[
                pltpu.VMEM((rows, pieces * rows), F32),
                pltpu.VMEM((rows, pieces * rows), BF16),
                pltpu.VMEM((pieces * rows, 2 * HD), BF16),
                pltpu.VMEM((HD, pieces * rows), F32),
            ],
        ),
        out_shape=[
            jax.ShapeDtypeStruct((rows, width), BF16),
            jax.ShapeDtypeStruct((rank, width), F32),
            jax.ShapeDtypeStruct((rank, rows), F32),
            jax.ShapeDtypeStruct((rank, pieces * rows), F32),
            jax.ShapeDtypeStruct((rank, kv * HD), F32),
        ],
        compiler_params=pltpu.CompilerParams(vmem_limit_bytes=50 * 2**20),
        cost_estimate=pl.CostEstimate(
            flops=10 * pairs * HD, bytes_accessed=16 * rows * width, transcendentals=pairs
        ),
    )(where, frozen, low_q, low_q_t, up_q, up_v, low_v, grad_out, *keys, *values)


class Routes:
    def __init__(self, blocks):
        self.seq = lax.axis_size("seq")
        self.tensor = lax.axis_size("tensor")
        self.half = blocks // 2
        self.y = blocks // 4

    def upper(self, s, t):
        offset = self.half if t >= self.tensor // 2 else 0
        return ((s - offset) // self.half) % 2 == 1

    def send(self, block, target):
        route = []
        for s in range(self.seq):
            for t in range(self.tensor):
                to = target(s, t)
                if to is not None:
                    route.append((s * self.tensor + t, to % self.seq * self.tensor + t))
        return lax.ppermute(block, AXES, route)

    def core(self, block):
        return self.send(block, lambda s, t: s ^ 1)

    def across_y(self, block):
        return self.send(block, lambda s, t: s ^ self.y)

    def own_across_y(self, block):
        return self.send(
            block, lambda s, t: None if self.upper(s, t) and s & self.y else s ^ self.y
        )

    def up(self, block):
        return self.send(block, lambda s, t: None if self.upper(s, t) else s + self.half)

    def within_upper(self, block):
        return self.send(block, lambda s, t: s ^ self.y if self.upper(s, t) else None)

    def down(self, block):
        return self.send(block, lambda s, t: s - self.half if self.upper(s, t) else None)


def gather_blocks(routes, own):
    cut = own.shape[0] // 2 // 16 * 16
    from_y = routes.own_across_y(own)
    from_z = routes.up(own)
    first = routes.up(from_y[:cut])
    second = routes.within_upper(from_z[cut:])
    from_both = jnp.concatenate((first, second), axis=0)
    mine = (own, from_y, from_z, from_both)
    found = []
    for block in mine:
        found += [block, routes.core(block)]
    return found


def sum_over_tensor(part):
    size = lax.axis_size("tensor")
    step = 1
    while step < size:
        part = part + lax.ppermute(part, "tensor", [(i, i ^ step) for i in range(size)])
        step *= 2
    return part


def sum_over_seq(part):
    size = lax.axis_size("seq")
    odd = lax.axis_index("seq") % 2 == 1
    half = part.shape[1] // 2
    low, high = part[:, :half], part[:, half:]
    got = lax.ppermute(jnp.where(odd, low, high), "seq", [(i, i ^ 1) for i in range(size)])
    total = jnp.where(odd, high, low).astype(F32) + got.astype(F32)
    step = 2
    while step < size:
        sent = total.astype(BF16)
        got = lax.ppermute(sent, "seq", [(i, i ^ step) for i in range(size)])
        total = sent.astype(F32) + got.astype(F32)
        step *= 2
    total = total.astype(BF16)
    got = lax.ppermute(total, "seq", [(i, i ^ 1) for i in range(size)])
    return jnp.concatenate((jnp.where(odd, got, total), jnp.where(odd, total, got)), axis=1)


def per_device(
    hidden_in,
    frozen_query,
    key_base,
    frozen_value,
    down_query,
    query_upper_factor,
    down_value,
    value_upper_factor,
    grad_output,
):
    rows = hidden_in.shape[0]
    rank = down_query.shape[1]
    width_here = hidden_in.shape[1]
    kv_width = key_base.shape[1]
    blocks = GROUP // rows
    assert blocks == 8 and rows % 32 == 0
    routes = Routes(blocks)
    seq_at, tensor_at = lax.axis_index("seq"), lax.axis_index("tensor")
    offset = jnp.where(tensor_at >= lax.axis_size("tensor") // 2, routes.half, 0)
    place = (seq_at - offset) % blocks
    where = jnp.stack([place % 2, place // routes.y % 2, place // routes.half]).astype(jnp.int32)

    keys = gather_blocks(routes, key_base)
    down = jnp.concatenate((down_query, down_value), axis=1)
    part_t = lax.dot_general(down, hidden_in, (((0,), (1,)), ((), ())), preferred_element_type=F32)
    low_t = sum_over_tensor(part_t).astype(BF16)
    low_q_t, low_v_t = low_t[:rank], low_t[rank:]
    low_q = low_q_t.T
    value_rows = (
        frozen_value.astype(F32)
        + ADAPTER_SCALE
        * lax.dot_general(
            low_v_t, value_upper_factor, (((0,), (0,)), ((), ())), preferred_element_type=F32
        )
    ).astype(BF16)
    low_rows = low_v_t.reshape(rank * rows // kv_width, kv_width)
    extra = -(-low_rows.shape[0] // 16) * 16
    low_rows = jnp.pad(low_rows, ((0, extra - low_rows.shape[0]), (0, 0)))
    packed = gather_blocks(routes, jnp.concatenate((value_rows, low_rows), axis=0))
    low_v = jnp.concatenate(
        [p[rows : rows + rank * rows // kv_width].reshape(rank, rows) for p in packed], axis=1
    )

    attention, grad_up_q, back_q, back_v, grad_up_v = attention_call(
        where,
        frozen_query,
        low_q,
        low_q_t,
        query_upper_factor,
        value_upper_factor,
        low_v,
        grad_output,
        keys,
        packed,
    )

    back_v = back_v.reshape(rank, 4, 2, rows)
    mine = back_v[:, :, 0] + routes.core(back_v[:, :, 1])
    mine = mine[:, 0::2] + routes.across_y(mine[:, 1::2])
    mine = mine[:, 0] + routes.down(mine[:, 1])
    back = sum_over_tensor(jnp.concatenate((back_q, mine), axis=0)).astype(BF16)
    grad_down = dot(back, hidden_in, NN)

    summed = sum_over_seq(
        jnp.concatenate(
            (grad_down[:rank], grad_down[rank:], grad_up_q, grad_up_v), axis=1
        ).astype(BF16)
    ).astype(F32)
    grad_down_query = summed[:, :width_here].T
    grad_down_value = summed[:, width_here : 2 * width_here].T
    grad_up_query = summed[:, 2 * width_here : -kv_width]
    grad_up_value = summed[:, -kv_width:]
    return attention, grad_down_query, grad_up_query, grad_down_value, grad_up_value


def solution(mesh):
    placed = (
        P("seq", "tensor"),
        P("seq", "tensor"),
        P("seq", "tensor"),
        P("seq", "tensor"),
        P("tensor", None),
        P(None, "tensor"),
        P("tensor", None),
        P(None, "tensor"),
        P("seq", "tensor"),
    )
    return jax.shard_map(
        per_device,
        mesh=mesh,
        in_specs=placed,
        out_specs=(
            P("seq", "tensor"),
            P("tensor", None),
            P(None, "tensor"),
            P("tensor", None),
            P(None, "tensor"),
        ),
        check_vma=False,
    )
```

```python
import functools

import jax
import jax.numpy as jnp
from jax import lax
from jax.experimental import pallas as pl
from jax.experimental.pallas import tpu as pltpu
from jax.sharding import PartitionSpec as P

HD = 128
GROUP = 2048
ADAPTER_SCALE = 0.5
LOG2E = 1.4426950408889634
MASKED = -1e30

F32 = jnp.float32
BF16 = jnp.bfloat16
NN = (((1,), (0,)), ((), ()))
NT = (((1,), (1,)), ((), ()))

AXES = ("seq", "tensor")


def dot(a, b, dims):
    return lax.dot_general(a, b, dims, preferred_element_type=F32)


ONES = 16


def attention_body(rows, per_head, kv, stacked, where, *refs):
    frozen, low_q, low_q_t, up_q, up_v, low_v, grad_out = refs[:7]
    given = refs[7:17]
    out, grad_up_q, back_q, back_v, grad_up_v = refs[17:22]
    scores, probs, grad_s, keys, keys_t, values, values_t, grad_v = refs[22:]
    scale = float(HD) ** -0.5
    to_log2 = scale * LOG2E
    core, y_bit, z_bit = where[0], where[1], where[2]
    half = rows // 2
    parts = [(given[j], 0, rows) for j in range(6)]
    parts = [[p] for p in parts]
    parts += [[(given[6], 0, half), (given[7], half, half)], [(given[8], 0, half), (given[9], half, half)]]
    width_kv = kv * HD
    columns = stacked * rows
    steps = kv * per_head // stacked
    steps_per_kv = per_head // stacked
    back_q[...] = jnp.zeros_like(back_q)
    back_v[...] = jnp.zeros_like(back_v)
    key_at = lax.broadcasted_iota(jnp.int32, (rows, columns), 0)
    query_at = lax.broadcasted_iota(jnp.int32, (rows, columns), 1) % rows

    def prepare(blocks):
        for slot, j in enumerate(blocks):
            for ref, first, count in parts[j]:
                at = slice(slot * rows + first, slot * rows + first + count)
                low_at = slice(j * rows + first, j * rows + first + count)
                block = ref[:, :width_kv]
                keys[at, :] = block
                keys_t[:, at] = block.T
                added = lax.dot_general(
                    low_v[:, low_at], up_v[...], (((0,), (0,)), ((), ())), preferred_element_type=F32
                )
                block = (ref[:, width_kv:].astype(F32) + ADAPTER_SCALE * added).astype(BF16)
                values[at, :] = block
                block_t = block.T
                for g in range(kv):
                    values_t[g, :HD, at] = block_t[g * HD : (g + 1) * HD]
                    values_t[g, HD:, at] = jnp.ones((ONES, count), BF16)
                grad_v[at, :] = jnp.zeros((count, width_kv), F32)

    def finish(blocks):
        for g in range(kv):
            cols = slice(g * HD, (g + 1) * HD)
            total = None
            for slot, j in enumerate(blocks):
                rounded = grad_v[slot * rows : (slot + 1) * rows, cols].astype(BF16)
                at = slice(j * rows, (j + 1) * rows)
                back_v[:, at] += ADAPTER_SCALE * dot(up_v[:, cols], rounded, NT)
                term = dot(low_v[:, at], rounded, NN)
                total = term if total is None else total + term
            grad_up_v[:, cols] = ADAPTER_SCALE * total

    def attend(length, pipelined):
        def wide(i):
            return pl.ds(pl.multiple_of(i * (stacked * HD), stacked * HD), stacked * HD)

        def narrow(i, a):
            return pl.ds(pl.multiple_of(i * (stacked * HD) + a * HD, HD), HD)

        def kv_cols(i):
            return pl.ds(pl.multiple_of((i // steps_per_kv) * HD, HD), HD)

        def score(i, slot):
            query = frozen[:, wide(i)].astype(F32) + ADAPTER_SCALE * dot(low_q[...], up_q[:, wide(i)], NN)
            query = query.astype(BF16)
            query = jnp.concatenate([query[:, a * HD : (a + 1) * HD] for a in range(stacked)], axis=0)
            s = dot(keys[:length, kv_cols(i)], query, NT)
            own = jnp.where(key_at <= query_at, s[:rows], MASKED)
            sibling = jnp.where(core > 0, s[rows : 2 * rows], MASKED)
            scores[slot, :rows, :] = own
            scores[slot, rows : 2 * rows, :] = sibling
            top = jnp.max(jnp.maximum(own, sibling), axis=0, keepdims=True)
            if length > 2 * rows:
                rest = s[2 * rows :]
                scores[slot, 2 * rows : length, :] = rest
                top = jnp.maximum(top, jnp.max(rest, axis=0, keepdims=True))
            return top * to_log2

        def follow(i, slot, top):
            probs[:length, :] = jnp.exp2(scores[slot, :length, :] * to_log2 - top).astype(BF16)
            attended = dot(values_t[i // steps_per_kv, :, :length], probs[:length, :], NN)
            inverse = 1.0 / attended[HD : HD + 1, :]
            attended = (attended[:HD] * inverse).astype(BF16)
            for a in range(stacked):
                out[:, narrow(i, a)] = attended[:, a * rows : (a + 1) * rows].T
            upstream = jnp.concatenate([grad_out[:, narrow(i, a)].T for a in range(stacked)], axis=1)
            upstream_f = upstream.astype(F32)
            delta = jnp.sum(upstream_f * attended.astype(F32), axis=0, keepdims=True)
            normed = (upstream_f * inverse).astype(BF16)
            grad_probs = dot(values[:length, kv_cols(i)], upstream, NN)
            grad_s[:length, :] = (probs[:length, :].astype(F32) * (grad_probs - delta)).astype(BF16)
            grad_v[:length, kv_cols(i)] += dot(probs[:length, :], normed, NT)
            grad_query = dot(keys_t[kv_cols(i), :length], grad_s[:length, :], NN)
            grad_query = (grad_query * (inverse * scale)).astype(BF16)
            back = None
            for a in range(stacked):
                one = grad_query[:, a * rows : (a + 1) * rows]
                grad_up_q[:, narrow(i, a)] = ADAPTER_SCALE * dot(low_q_t[...], one, NT)
                term = dot(up_q[:, narrow(i, a)], one, NN)
                back = term if back is None else back + term
            back_q[...] += ADAPTER_SCALE * back

        if pipelined:

            def two_steps(t, top):
                for u in range(2):
                    i = 2 * t + u
                    later = score(jnp.minimum(i + 1, steps - 1), 1 - u)
                    follow(i, u, top)
                    top = later
                return top

            lax.fori_loop(0, steps // 2, two_steps, score(0, 0))
        else:

            def one_step(i, carry):
                follow(i, 0, score(i, 0))
                return carry

            lax.fori_loop(0, steps, one_step, 0)

    for y in (0, 1):
        for z in (0, 1):

            @pl.when((y_bit == y) & (z_bit == z))
            def _():
                blocks = [0, 1] + [2, 3] * y + [4, 5, 6, 7] * z
                prepare(blocks)
                attend(len(blocks) * rows, len(blocks) == 8 and steps % 2 == 0)
                finish(blocks)


def attention_call(where, frozen, low_q, low_q_t, up_q, up_v, low_v, grad_out, given):
    rows, width = frozen.shape
    kv = up_v.shape[1] // HD
    rank = up_q.shape[0]
    per_head = width // HD // kv
    reach = low_v.shape[1]
    stacked = 2
    vmem = pl.BlockSpec(memory_space=pltpu.VMEM)
    pairs = rows * reach * per_head * kv
    return pl.pallas_call(
        functools.partial(attention_body, rows, per_head, kv, stacked),
        in_specs=[pl.BlockSpec(memory_space=pltpu.SMEM)] + [vmem] * (7 + len(given)),
        out_specs=[vmem] * 5,
        scratch_shapes=[
            pltpu.VMEM((2, reach, stacked * rows), F32),
            pltpu.VMEM((reach, stacked * rows), BF16),
            pltpu.VMEM((reach, stacked * rows), BF16),
            pltpu.VMEM((reach, kv * HD), BF16),
            pltpu.VMEM((kv * HD, reach), BF16),
            pltpu.VMEM((reach, kv * HD), BF16),
            pltpu.VMEM((kv, HD + ONES, reach), BF16),
            pltpu.VMEM((reach, kv * HD), F32),
        ],
        out_shape=[
            jax.ShapeDtypeStruct((rows, width), BF16),
            jax.ShapeDtypeStruct((rank, width), F32),
            jax.ShapeDtypeStruct((rank, rows), F32),
            jax.ShapeDtypeStruct((rank, reach), F32),
            jax.ShapeDtypeStruct((rank, kv * HD), F32),
        ],
        compiler_params=pltpu.CompilerParams(vmem_limit_bytes=56 * 2**20),
        cost_estimate=pl.CostEstimate(
            flops=10 * pairs * HD, bytes_accessed=16 * rows * width, transcendentals=pairs
        ),
    )(where, frozen, low_q, low_q_t, up_q, up_v, low_v, grad_out, *given)


class Routes:
    def __init__(self, blocks):
        self.seq = lax.axis_size("seq")
        self.tensor = lax.axis_size("tensor")
        self.half = blocks // 2
        self.y = blocks // 4

    def upper(self, s, t):
        offset = self.half if t >= self.tensor // 2 else 0
        return ((s - offset) // self.half) % 2 == 1

    def send(self, block, target):
        route = []
        for s in range(self.seq):
            for t in range(self.tensor):
                to = target(s, t)
                if to is not None:
                    route.append((s * self.tensor + t, to % self.seq * self.tensor + t))
        return lax.ppermute(block, AXES, route)

    def core(self, block):
        return self.send(block, lambda s, t: s ^ 1)

    def across_y(self, block):
        return self.send(block, lambda s, t: s ^ self.y)

    def own_across_y(self, block):
        return self.send(
            block, lambda s, t: None if self.upper(s, t) and s & self.y else s ^ self.y
        )

    def up(self, block):
        return self.send(block, lambda s, t: None if self.upper(s, t) else s + self.half)

    def within_upper(self, block):
        return self.send(block, lambda s, t: s ^ self.y if self.upper(s, t) else None)

    def down(self, block):
        return self.send(block, lambda s, t: s - self.half if self.upper(s, t) else None)


def gather_blocks(routes, own):
    cut = own.shape[0] // 2
    from_y = routes.own_across_y(own)
    from_z = routes.up(own)
    first = routes.up(from_y[:cut])
    second = routes.within_upper(from_z[cut:])
    found = []
    for block in (own, from_y, from_z):
        found += [block, routes.core(block)]
    return found + [first, second, routes.core(first), routes.core(second)]


def gather_low(routes, own):
    near = jnp.concatenate((own, routes.across_y(own)), axis=1)
    mine = jnp.concatenate((near, routes.up(near)), axis=1)
    other = routes.core(mine)
    rank = own.shape[0]
    both = jnp.stack((mine.reshape(rank, 4, -1), other.reshape(rank, 4, -1)), axis=2)
    return both.reshape(rank, -1)


def sum_over_tensor(part):
    size = lax.axis_size("tensor")
    step = 1
    while step < size:
        part = part + lax.ppermute(part, "tensor", [(i, i ^ step) for i in range(size)])
        step *= 2
    return part


def sum_over_seq(part):
    size = lax.axis_size("seq")
    odd = lax.axis_index("seq") % 2 == 1
    half = part.shape[1] // 2
    low, high = part[:, :half], part[:, half:]
    got = lax.ppermute(jnp.where(odd, low, high), "seq", [(i, i ^ 1) for i in range(size)])
    total = jnp.where(odd, high, low).astype(F32) + got.astype(F32)
    step = 2
    while step < size:
        sent = total.astype(BF16)
        got = lax.ppermute(sent, "seq", [(i, i ^ step) for i in range(size)])
        total = sent.astype(F32) + got.astype(F32)
        step *= 2
    total = total.astype(BF16)
    got = lax.ppermute(total, "seq", [(i, i ^ 1) for i in range(size)])
    return jnp.concatenate((jnp.where(odd, got, total), jnp.where(odd, total, got)), axis=1)


def per_device(
    hidden_in,
    frozen_query,
    key_base,
    frozen_value,
    down_query,
    query_upper_factor,
    down_value,
    value_upper_factor,
    grad_output,
):
    rows = hidden_in.shape[0]
    rank = down_query.shape[1]
    width_here = hidden_in.shape[1]
    kv_width = key_base.shape[1]
    blocks = GROUP // rows
    assert blocks == 8 and rows % 32 == 0
    routes = Routes(blocks)
    seq_at, tensor_at = lax.axis_index("seq"), lax.axis_index("tensor")
    offset = jnp.where(tensor_at >= lax.axis_size("tensor") // 2, routes.half, 0)
    place = (seq_at - offset) % blocks
    where = jnp.stack([place % 2, place // routes.y % 2, place // routes.half]).astype(jnp.int32)

    given = gather_blocks(routes, jnp.concatenate((key_base, frozen_value), axis=1))
    down = jnp.concatenate((down_query, down_value), axis=1)
    part_t = lax.dot_general(down, hidden_in, (((0,), (1,)), ((), ())), preferred_element_type=F32)
    low_t = sum_over_tensor(part_t).astype(BF16)
    low_q_t = low_t[:rank]
    low_v = gather_low(routes, low_t[rank:])

    attention, grad_up_q, back_q, back_v, grad_up_v = attention_call(
        where,
        frozen_query,
        low_q_t.T,
        low_q_t,
        query_upper_factor,
        value_upper_factor,
        low_v,
        grad_output,
        given,
    )

    back_v = back_v.reshape(rank, 4, 2, rows)
    mine = back_v[:, :, 0] + routes.core(back_v[:, :, 1])
    mine = mine[:, 0::2] + routes.across_y(mine[:, 1::2])
    mine = mine[:, 0] + routes.down(mine[:, 1])
    back = sum_over_tensor(jnp.concatenate((back_q, mine), axis=0)).astype(BF16)
    grad_down = dot(back, hidden_in, NN)

    summed = sum_over_seq(
        jnp.concatenate(
            (grad_down[:rank], grad_down[rank:], grad_up_q, grad_up_v), axis=1
        ).astype(BF16)
    ).astype(F32)
    grad_down_query = summed[:, :width_here].T
    grad_down_value = summed[:, width_here : 2 * width_here].T
    grad_up_query = summed[:, 2 * width_here : -kv_width]
    grad_up_value = summed[:, -kv_width:]
    return attention, grad_down_query, grad_up_query, grad_down_value, grad_up_value


def solution(mesh):
    placed = (
        P("seq", "tensor"),
        P("seq", "tensor"),
        P("seq", "tensor"),
        P("seq", "tensor"),
        P("tensor", None),
        P(None, "tensor"),
        P("tensor", None),
        P(None, "tensor"),
        P("seq", "tensor"),
    )
    return jax.shard_map(
        per_device,
        mesh=mesh,
        in_specs=placed,
        out_specs=(
            P("seq", "tensor"),
            P("tensor", None),
            P(None, "tensor"),
            P("tensor", None),
            P(None, "tensor"),
        ),
        check_vma=False,
    )
```

```python
import functools

import jax
import jax.numpy as jnp
from jax import lax
from jax.experimental import pallas as pl
from jax.experimental.pallas import tpu as pltpu
from jax.sharding import PartitionSpec as P

HD = 128
GROUP = 2048
ADAPTER_SCALE = 0.5
LOG2E = 1.4426950408889634
MASKED = -1e30

F32 = jnp.float32
BF16 = jnp.bfloat16
NN = (((1,), (0,)), ((), ()))
NT = (((1,), (1,)), ((), ()))

AXES = ("seq", "tensor")


def dot(a, b, dims):
    return lax.dot_general(a, b, dims, preferred_element_type=F32)


def place_in_group(blocks):
    shifted = lax.axis_index("tensor") >= lax.axis_size("tensor") // 2
    return (lax.axis_index("seq") + jnp.where(shifted, blocks // 2, 0)) % blocks


ONES = 16


def attention_body(rows, per_head, kv, stacked, blocks_in_group, *refs):
    frozen, low_q_t, up_q, up_v, grad_out = refs[:5]
    low_v = refs[5:9]
    given = refs[9:19]
    out, grad_up_q, back_q, back_v, back_v_sibling, grad_up_v = refs[19:25]
    low_q, scores, probs, grad_s, keys, keys_t, values, values_t, grad_v = refs[25:]
    scale = float(HD) ** -0.5
    to_log2 = scale * LOG2E
    place = place_in_group(blocks_in_group)
    core, y_bit, z_bit = place % 2, place // (blocks_in_group // 4) % 2, place // (blocks_in_group // 2)
    half = rows // 2
    parts = [(given[j], 0, rows) for j in range(6)]
    parts = [[p] for p in parts]
    parts += [[(given[6], 0, half), (given[7], half, half)], [(given[8], 0, half), (given[9], half, half)]]
    width_kv = kv * HD
    columns = stacked * rows
    steps = kv * per_head // stacked
    steps_per_kv = per_head // stacked
    back_q[...] = jnp.zeros_like(back_q)
    back_v[...] = jnp.zeros_like(back_v)
    back_v_sibling[...] = jnp.zeros_like(back_v)
    low_q[...] = low_q_t[...].T
    key_at = lax.broadcasted_iota(jnp.int32, (rows, columns), 0)
    query_at = lax.broadcasted_iota(jnp.int32, (rows, columns), 1) % rows

    def prepare(blocks):
        for slot, j in enumerate(blocks):
            for ref, first, count in parts[j]:
                at = slice(slot * rows + first, slot * rows + first + count)
                low_at = slice(j % 2 * rows + first, j % 2 * rows + first + count)
                block = ref[:, :width_kv]
                keys[at, :] = block
                keys_t[:, at] = block.T
                added = lax.dot_general(
                    low_v[j // 2][:, low_at], up_v[...], (((0,), (0,)), ((), ())), preferred_element_type=F32
                )
                block = (ref[:, width_kv:].astype(F32) + ADAPTER_SCALE * added).astype(BF16)
                values[at, :] = block
                block_t = block.T
                for g in range(kv):
                    values_t[g, :HD, at] = block_t[g * HD : (g + 1) * HD]
                    values_t[g, HD:, at] = jnp.ones((ONES, count), BF16)
                grad_v[at, :] = jnp.zeros((count, width_kv), F32)

    def finish(blocks):
        for g in range(kv):
            cols = slice(g * HD, (g + 1) * HD)
            total = None
            for slot, j in enumerate(blocks):
                rounded = grad_v[slot * rows : (slot + 1) * rows, cols].astype(BF16)
                at = slice(j // 2 * rows, (j // 2 + 1) * rows)
                target = back_v_sibling if j % 2 else back_v
                target[:, at] += ADAPTER_SCALE * dot(up_v[:, cols], rounded, NT)
                term = dot(low_v[j // 2][:, j % 2 * rows : (j % 2 + 1) * rows], rounded, NN)
                total = term if total is None else total + term
            grad_up_v[:, cols] = (ADAPTER_SCALE * total).astype(BF16)

    def attend(length, pipelined):
        def wide(i):
            return pl.ds(pl.multiple_of(i * (stacked * HD), stacked * HD), stacked * HD)

        def narrow(i, a):
            return pl.ds(pl.multiple_of(i * (stacked * HD) + a * HD, HD), HD)

        def kv_cols(i):
            return pl.ds(pl.multiple_of((i // steps_per_kv) * HD, HD), HD)

        def score(i, slot):
            query = frozen[:, wide(i)].astype(F32) + ADAPTER_SCALE * dot(low_q[...], up_q[:, wide(i)], NN)
            query = query.astype(BF16)
            query = jnp.concatenate([query[:, a * HD : (a + 1) * HD] for a in range(stacked)], axis=0)
            s = dot(keys[:length, kv_cols(i)], query, NT)
            own = jnp.where(key_at <= query_at, s[:rows], MASKED)
            sibling = jnp.where(core > 0, s[rows : 2 * rows], MASKED)
            scores[slot, :rows, :] = own
            scores[slot, rows : 2 * rows, :] = sibling
            top = jnp.max(jnp.maximum(own, sibling), axis=0, keepdims=True)
            if length > 2 * rows:
                rest = s[2 * rows :]
                scores[slot, 2 * rows : length, :] = rest
                top = jnp.maximum(top, jnp.max(rest, axis=0, keepdims=True))
            return top * to_log2

        def follow(i, slot, top):
            probs[:length, :] = jnp.exp2(scores[slot, :length, :] * to_log2 - top).astype(BF16)
            attended = dot(values_t[i // steps_per_kv, :, :length], probs[:length, :], NN)
            inverse = 1.0 / attended[HD : HD + 1, :]
            attended = (attended[:HD] * inverse).astype(BF16)
            for a in range(stacked):
                out[:, narrow(i, a)] = attended[:, a * rows : (a + 1) * rows].T
            upstream = jnp.concatenate([grad_out[:, narrow(i, a)].T for a in range(stacked)], axis=1)
            upstream_f = upstream.astype(F32)
            delta = jnp.sum(upstream_f * attended.astype(F32), axis=0, keepdims=True)
            normed = (upstream_f * inverse).astype(BF16)
            grad_probs = dot(values[:length, kv_cols(i)], upstream, NN)
            grad_s[:length, :] = (probs[:length, :].astype(F32) * (grad_probs - delta)).astype(BF16)
            grad_v[:length, kv_cols(i)] += dot(probs[:length, :], normed, NT)
            grad_query = dot(keys_t[kv_cols(i), :length], grad_s[:length, :], NN)
            grad_query = (grad_query * (inverse * scale)).astype(BF16)
            back = None
            for a in range(stacked):
                one = grad_query[:, a * rows : (a + 1) * rows]
                grad_up_q[:, narrow(i, a)] = (ADAPTER_SCALE * dot(low_q_t[...], one, NT)).astype(BF16)
                term = dot(up_q[:, narrow(i, a)], one, NN)
                back = term if back is None else back + term
            back_q[...] += ADAPTER_SCALE * back

        if pipelined:

            def two_steps(t, top):
                for u in range(2):
                    i = 2 * t + u
                    later = score(jnp.minimum(i + 1, steps - 1), 1 - u)
                    follow(i, u, top)
                    top = later
                return top

            lax.fori_loop(0, steps // 2, two_steps, score(0, 0))
        else:

            def one_step(i, carry):
                follow(i, 0, score(i, 0))
                return carry

            lax.fori_loop(0, steps, one_step, 0)

    for y in (0, 1):
        for z in (0, 1):

            @pl.when((y_bit == y) & (z_bit == z))
            def _():
                blocks = [0, 1] + [2, 3] * y + [4, 5, 6, 7] * z
                prepare(blocks)
                attend(len(blocks) * rows, len(blocks) == 8 and steps % 2 == 0)
                finish(blocks)


def attention_call(frozen, low_q_t, up_q, up_v, grad_out, low_v, given):
    rows, width = frozen.shape
    kv = up_v.shape[1] // HD
    rank = up_q.shape[0]
    per_head = width // HD // kv
    reach = GROUP
    stacked = 2
    vmem = pl.BlockSpec(memory_space=pltpu.VMEM)
    pairs = rows * reach * per_head * kv
    return pl.pallas_call(
        functools.partial(attention_body, rows, per_head, kv, stacked, GROUP // rows),
        in_specs=[vmem] * (5 + len(low_v) + len(given)),
        out_specs=[vmem] * 6,
        scratch_shapes=[
            pltpu.VMEM((rows, rank), BF16),
            pltpu.VMEM((2, reach, stacked * rows), F32),
            pltpu.VMEM((reach, stacked * rows), BF16),
            pltpu.VMEM((reach, stacked * rows), BF16),
            pltpu.VMEM((reach, kv * HD), BF16),
            pltpu.VMEM((kv * HD, reach), BF16),
            pltpu.VMEM((reach, kv * HD), BF16),
            pltpu.VMEM((kv, HD + ONES, reach), BF16),
            pltpu.VMEM((reach, kv * HD), F32),
        ],
        out_shape=[
            jax.ShapeDtypeStruct((rows, width), BF16),
            jax.ShapeDtypeStruct((rank, width), BF16),
            jax.ShapeDtypeStruct((rank, rows), F32),
            jax.ShapeDtypeStruct((rank, reach // 2), F32),
            jax.ShapeDtypeStruct((rank, reach // 2), F32),
            jax.ShapeDtypeStruct((rank, kv * HD), BF16),
        ],
        compiler_params=pltpu.CompilerParams(vmem_limit_bytes=56 * 2**20),
        cost_estimate=pl.CostEstimate(
            flops=10 * pairs * HD, bytes_accessed=16 * rows * width, transcendentals=pairs
        ),
    )(frozen, low_q_t, up_q, up_v, grad_out, *low_v, *given)


class Routes:
    def __init__(self, blocks):
        self.seq = lax.axis_size("seq")
        self.tensor = lax.axis_size("tensor")
        self.half = blocks // 2
        self.y = blocks // 4

    def upper(self, s, t):
        offset = self.half if t >= self.tensor // 2 else 0
        return ((s - offset) // self.half) % 2 == 1

    def send(self, block, target):
        route = []
        for s in range(self.seq):
            for t in range(self.tensor):
                to = target(s, t)
                if to is not None:
                    route.append((s * self.tensor + t, to % self.seq * self.tensor + t))
        return lax.ppermute(block, AXES, route)

    def core(self, block):
        return self.send(block, lambda s, t: s ^ 1)

    def across_y(self, block):
        return self.send(block, lambda s, t: s ^ self.y)

    def own_across_y(self, block):
        return self.send(
            block, lambda s, t: None if self.upper(s, t) and s & self.y else s ^ self.y
        )

    def up(self, block):
        return self.send(block, lambda s, t: None if self.upper(s, t) else s + self.half)

    def up_across_y(self, block):
        return self.send(
            block, lambda s, t: None if self.upper(s, t) else (s + self.half) ^ self.y
        )

    def within_upper(self, block):
        return self.send(block, lambda s, t: s ^ self.y if self.upper(s, t) else None)

    def down(self, block):
        return self.send(block, lambda s, t: s - self.half if self.upper(s, t) else None)


def gather_blocks(routes, own):
    cut = own.shape[0] // 2
    from_y = routes.own_across_y(own)
    from_z = routes.up(own)
    first = routes.up(from_y[:cut])
    second = routes.within_upper(from_z[cut:])
    found = []
    for block in (own, from_y, from_z):
        found += [block, routes.core(block)]
    return found + [first, second, routes.core(first), routes.core(second)]


def gather_low(routes, own):
    both = jnp.concatenate((own, routes.core(own)), axis=1)
    return [both, routes.across_y(both), routes.up(both), routes.up_across_y(both)]


def sum_over_tensor(part):
    size = lax.axis_size("tensor")
    step = 1
    while step < size:
        part = part + lax.ppermute(part, "tensor", [(i, i ^ step) for i in range(size)])
        step *= 2
    return part


def swap(block, step):
    return lax.ppermute(block, "seq", [(i, i ^ step) for i in range(lax.axis_size("seq"))])


def split_for_core(part):
    odd = lax.axis_index("seq") % 2 == 1
    half = part.shape[1] // 2
    low, high = part[:, :half], part[:, half:]
    return jnp.where(odd, high, low), jnp.where(odd, low, high)


def join_cores(total):
    odd = lax.axis_index("seq") % 2 == 1
    got = swap(total, 1)
    return jnp.concatenate((jnp.where(odd, got, total), jnp.where(odd, total, got)), axis=1)


def add_up(mine, got):
    return (mine.astype(F32) + got.astype(F32)).astype(BF16)


def sum_over_seq(part):
    kept, sent = split_for_core(part)
    total = add_up(kept, swap(sent, 1))
    step = 2
    while step < lax.axis_size("seq"):
        total = add_up(total, swap(total, step))
        step *= 2
    return join_cores(total)


def per_device(
    hidden_in,
    frozen_query,
    key_base,
    frozen_value,
    down_query,
    query_upper_factor,
    down_value,
    value_upper_factor,
    grad_output,
):
    rows = hidden_in.shape[0]
    rank = down_query.shape[1]
    width_here = hidden_in.shape[1]
    kv_width = key_base.shape[1]
    blocks = GROUP // rows
    assert blocks == 8 and rows % 32 == 0
    routes = Routes(blocks)
    given = gather_blocks(routes, jnp.concatenate((key_base, frozen_value), axis=1))
    down = jnp.concatenate((down_query, down_value), axis=1)
    part_t = lax.dot_general(down, hidden_in, (((0,), (1,)), ((), ())), preferred_element_type=F32)
    low_t = sum_over_tensor(part_t).astype(BF16)
    low_q_t = low_t[:rank]
    low_v = gather_low(routes, low_t[rank:])

    attention, grad_up_q, back_q, back_v, back_v_sibling, grad_up_v = attention_call(
        frozen_query,
        low_q_t,
        query_upper_factor,
        value_upper_factor,
        grad_output,
        low_v,
        given,
    )

    grad_up = sum_over_seq(jnp.concatenate((grad_up_q, grad_up_v), axis=1)).astype(F32)
    back_v = (back_v + routes.core(back_v_sibling)).reshape(rank, 4, rows)
    back_v = back_v[:, 0::2] + routes.across_y(back_v[:, 1::2])
    back_v = back_v[:, 0] + routes.down(back_v[:, 1])
    back = sum_over_tensor(jnp.concatenate((back_q, back_v), axis=0)).astype(BF16)
    grad_down = dot(back, hidden_in, NN).astype(BF16)
    grad_down = sum_over_seq(jnp.concatenate((grad_down[:rank], grad_down[rank:]), axis=1))
    grad_down = grad_down.astype(F32)
    return (
        attention,
        grad_down[:, :width_here].T,
        grad_up[:, :-kv_width],
        grad_down[:, width_here:].T,
        grad_up[:, -kv_width:],
    )


def solution(mesh):
    placed = (
        P("seq", "tensor"),
        P("seq", "tensor"),
        P("seq", "tensor"),
        P("seq", "tensor"),
        P("tensor", None),
        P(None, "tensor"),
        P("tensor", None),
        P(None, "tensor"),
        P("seq", "tensor"),
    )
    return jax.shard_map(
        per_device,
        mesh=mesh,
        in_specs=placed,
        out_specs=(
            P("seq", "tensor"),
            P("tensor", None),
            P(None, "tensor"),
            P("tensor", None),
            P(None, "tensor"),
        ),
        check_vma=False,
    )
```

```python
import functools

import jax
import jax.numpy as jnp
from jax import lax
from jax.experimental import pallas as pl
from jax.experimental.pallas import tpu as pltpu
from jax.sharding import PartitionSpec as P

HD = 128
GROUP = 2048
ADAPTER_SCALE = 0.5
LOG2E = 1.4426950408889634
MASKED = -1e30
VMEM_LIMIT = 40

F32 = jnp.float32
BF16 = jnp.bfloat16
NN = (((1,), (0,)), ((), ()))
NT = (((1,), (1,)), ((), ()))

AXES = ("seq", "tensor")


def dot(a, b, dims):
    return lax.dot_general(a, b, dims, preferred_element_type=F32)


def place_in_group(blocks):
    shifted = lax.axis_index("tensor") >= lax.axis_size("tensor") // 2
    return (lax.axis_index("seq") + jnp.where(shifted, blocks // 2, 0)) % blocks


ONES = 16


def attention_body(rows, per_head, kv, stacked, blocks_in_group, *refs):
    frozen, low_q_t, up_q, up_v, grad_out = refs[:5]
    low_v = refs[5:9]
    given = refs[9:19]
    out, grad_up_q, back_q, back_v, back_v_sibling, grad_up_v = refs[19:25]
    low_q, scores, probs, grad_s, keys, keys_t, values, values_t, grad_v = refs[25:]
    scale = float(HD) ** -0.5
    to_log2 = scale * LOG2E
    place = place_in_group(blocks_in_group)
    core, y_bit, z_bit = place % 2, place // (blocks_in_group // 4) % 2, place // (blocks_in_group // 2)
    half = rows // 2
    parts = [(given[j], 0, rows) for j in range(6)]
    parts = [[p] for p in parts]
    parts += [[(given[6], 0, half), (given[7], half, half)], [(given[8], 0, half), (given[9], half, half)]]
    width_kv = kv * HD
    columns = stacked * rows
    steps = kv * per_head // stacked
    steps_per_kv = per_head // stacked
    back_q[...] = jnp.zeros_like(back_q)
    back_v[...] = jnp.zeros_like(back_v)
    back_v_sibling[...] = jnp.zeros_like(back_v)
    low_q[...] = low_q_t[...].T
    key_at = lax.broadcasted_iota(jnp.int32, (rows, columns), 0)
    query_at = lax.broadcasted_iota(jnp.int32, (rows, columns), 1) % rows

    def prepare(blocks):
        for slot, j in enumerate(blocks):
            for ref, first, count in parts[j]:
                at = slice(slot * rows + first, slot * rows + first + count)
                low_at = slice(j % 2 * rows + first, j % 2 * rows + first + count)
                block = ref[:, :width_kv]
                keys[at, :] = block
                keys_t[:, at] = block.T
                added = lax.dot_general(
                    low_v[j // 2][:, low_at], up_v[...], (((0,), (0,)), ((), ())), preferred_element_type=F32
                )
                block = (ref[:, width_kv:].astype(F32) + ADAPTER_SCALE * added).astype(BF16)
                values[at, :] = block
                block_t = block.T
                for g in range(kv):
                    values_t[g, :HD, at] = block_t[g * HD : (g + 1) * HD]
                    values_t[g, HD:, at] = jnp.ones((ONES, count), BF16)
                grad_v[at, :] = jnp.zeros((count, width_kv), F32)

    def finish(blocks):
        for g in range(kv):
            cols = slice(g * HD, (g + 1) * HD)
            total = None
            for slot, j in enumerate(blocks):
                rounded = grad_v[slot * rows : (slot + 1) * rows, cols].astype(BF16)
                at = slice(j // 2 * rows, (j // 2 + 1) * rows)
                target = back_v_sibling if j % 2 else back_v
                target[:, at] += ADAPTER_SCALE * dot(up_v[:, cols], rounded, NT)
                term = dot(low_v[j // 2][:, j % 2 * rows : (j % 2 + 1) * rows], rounded, NN)
                total = term if total is None else total + term
            grad_up_v[:, cols] = (ADAPTER_SCALE * total).astype(BF16)

    def attend(length):
        def wide(i):
            return pl.ds(pl.multiple_of(i * (stacked * HD), stacked * HD), stacked * HD)

        def narrow(i, a):
            return pl.ds(pl.multiple_of(i * (stacked * HD) + a * HD, HD), HD)

        def kv_cols(i):
            return pl.ds(pl.multiple_of((i // steps_per_kv) * HD, HD), HD)

        def score(i):
            query = frozen[:, wide(i)].astype(F32) + ADAPTER_SCALE * dot(low_q[...], up_q[:, wide(i)], NN)
            query = query.astype(BF16)
            query = jnp.concatenate([query[:, a * HD : (a + 1) * HD] for a in range(stacked)], axis=0)
            s = dot(keys[:length, kv_cols(i)], query, NT)
            own = jnp.where(key_at <= query_at, s[:rows], MASKED)
            sibling = jnp.where(core > 0, s[rows : 2 * rows], MASKED)
            scores[:rows, :] = own
            scores[rows : 2 * rows, :] = sibling
            top = jnp.max(jnp.maximum(own, sibling), axis=0, keepdims=True)
            if length > 2 * rows:
                rest = s[2 * rows :]
                scores[2 * rows : length, :] = rest
                top = jnp.maximum(top, jnp.max(rest, axis=0, keepdims=True))
            return top * to_log2

        def one_step(i, top):
            probs[:length, :] = jnp.exp2(scores[:length, :] * to_log2 - top).astype(BF16)
            later = score(jnp.minimum(i + 1, steps - 1))
            attended = dot(values_t[i // steps_per_kv, :, :length], probs[:length, :], NN)
            inverse = 1.0 / attended[HD : HD + 1, :]
            attended = (attended[:HD] * inverse).astype(BF16)
            for a in range(stacked):
                out[:, narrow(i, a)] = attended[:, a * rows : (a + 1) * rows].T
            upstream = jnp.concatenate([grad_out[:, narrow(i, a)].T for a in range(stacked)], axis=1)
            upstream_f = upstream.astype(F32)
            delta = jnp.sum(upstream_f * attended.astype(F32), axis=0, keepdims=True)
            normed = (upstream_f * inverse).astype(BF16)
            grad_probs = dot(values[:length, kv_cols(i)], upstream, NN)
            grad_s[:length, :] = (probs[:length, :].astype(F32) * (grad_probs - delta)).astype(BF16)
            grad_v[:length, kv_cols(i)] += dot(probs[:length, :], normed, NT)
            grad_query = dot(keys_t[kv_cols(i), :length], grad_s[:length, :], NN)
            grad_query = (grad_query * (inverse * scale)).astype(BF16)
            back = None
            for a in range(stacked):
                one = grad_query[:, a * rows : (a + 1) * rows]
                grad_up_q[:, narrow(i, a)] = (ADAPTER_SCALE * dot(low_q_t[...], one, NT)).astype(BF16)
                term = dot(up_q[:, narrow(i, a)], one, NN)
                back = term if back is None else back + term
            back_q[...] += ADAPTER_SCALE * back

            return later

        lax.fori_loop(0, steps, one_step, score(0))

    for y in (0, 1):
        for z in (0, 1):

            @pl.when((y_bit == y) & (z_bit == z))
            def _():
                blocks = [0, 1] + [2, 3] * y + [4, 5, 6, 7] * z
                prepare(blocks)
                attend(len(blocks) * rows)
                finish(blocks)


def attention_call(frozen, low_q_t, up_q, up_v, grad_out, low_v, given):
    rows, width = frozen.shape
    kv = up_v.shape[1] // HD
    rank = up_q.shape[0]
    per_head = width // HD // kv
    reach = GROUP
    stacked = 2
    vmem = pl.BlockSpec(memory_space=pltpu.VMEM)
    pairs = rows * reach * per_head * kv
    return pl.pallas_call(
        functools.partial(attention_body, rows, per_head, kv, stacked, GROUP // rows),
        in_specs=[vmem] * (5 + len(low_v) + len(given)),
        out_specs=[vmem] * 6,
        scratch_shapes=[
            pltpu.VMEM((rows, rank), BF16),
            pltpu.VMEM((reach, stacked * rows), F32),
            pltpu.VMEM((reach, stacked * rows), BF16),
            pltpu.VMEM((reach, stacked * rows), BF16),
            pltpu.VMEM((reach, kv * HD), BF16),
            pltpu.VMEM((kv * HD, reach), BF16),
            pltpu.VMEM((reach, kv * HD), BF16),
            pltpu.VMEM((kv, HD + ONES, reach), BF16),
            pltpu.VMEM((reach, kv * HD), F32),
        ],
        out_shape=[
            jax.ShapeDtypeStruct((rows, width), BF16),
            jax.ShapeDtypeStruct((rank, width), BF16),
            jax.ShapeDtypeStruct((rank, rows), F32),
            jax.ShapeDtypeStruct((rank, reach // 2), F32),
            jax.ShapeDtypeStruct((rank, reach // 2), F32),
            jax.ShapeDtypeStruct((rank, kv * HD), BF16),
        ],
        compiler_params=pltpu.CompilerParams(vmem_limit_bytes=VMEM_LIMIT * 2**20),
        cost_estimate=pl.CostEstimate(
            flops=10 * pairs * HD, bytes_accessed=16 * rows * width, transcendentals=pairs
        ),
    )(frozen, low_q_t, up_q, up_v, grad_out, *low_v, *given)


class Routes:
    def __init__(self, blocks):
        self.seq = lax.axis_size("seq")
        self.tensor = lax.axis_size("tensor")
        self.half = blocks // 2
        self.y = blocks // 4

    def upper(self, s, t):
        offset = self.half if t >= self.tensor // 2 else 0
        return ((s - offset) // self.half) % 2 == 1

    def send(self, block, target):
        route = []
        for s in range(self.seq):
            for t in range(self.tensor):
                to = target(s, t)
                if to is not None:
                    route.append((s * self.tensor + t, to % self.seq * self.tensor + t))
        return lax.ppermute(block, AXES, route)

    def core(self, block):
        return self.send(block, lambda s, t: s ^ 1)

    def across_y(self, block):
        return self.send(block, lambda s, t: s ^ self.y)

    def own_across_y(self, block):
        return self.send(
            block, lambda s, t: None if self.upper(s, t) and s & self.y else s ^ self.y
        )

    def up(self, block):
        return self.send(block, lambda s, t: None if self.upper(s, t) else s + self.half)

    def up_across_y(self, block):
        return self.send(
            block, lambda s, t: None if self.upper(s, t) else (s + self.half) ^ self.y
        )

    def within_upper(self, block):
        return self.send(block, lambda s, t: s ^ self.y if self.upper(s, t) else None)

    def down(self, block):
        return self.send(block, lambda s, t: s - self.half if self.upper(s, t) else None)


def gather_blocks(routes, own):
    cut = own.shape[0] // 2
    from_y = routes.own_across_y(own)
    from_z = routes.up(own)
    first = routes.up(from_y[:cut])
    second = routes.within_upper(from_z[cut:])
    found = []
    for block in (own, from_y, from_z):
        found += [block, routes.core(block)]
    return found + [first, second, routes.core(first), routes.core(second)]


def gather_low(routes, own):
    both = jnp.concatenate((own, routes.core(own)), axis=1)
    return [both, routes.across_y(both), routes.up(both), routes.up_across_y(both)]


def sum_over_tensor(part):
    size = lax.axis_size("tensor")
    step = 1
    while step < size:
        part = part + lax.ppermute(part, "tensor", [(i, i ^ step) for i in range(size)])
        step *= 2
    return part


def swap(block, step):
    return lax.ppermute(block, "seq", [(i, i ^ step) for i in range(lax.axis_size("seq"))])


def split_for_core(part):
    odd = lax.axis_index("seq") % 2 == 1
    half = part.shape[1] // 2
    low, high = part[:, :half], part[:, half:]
    return jnp.where(odd, high, low), jnp.where(odd, low, high)


def join_cores(total):
    odd = lax.axis_index("seq") % 2 == 1
    got = swap(total, 1)
    return jnp.concatenate((jnp.where(odd, got, total), jnp.where(odd, total, got)), axis=1)


def add_up(mine, got):
    return (mine.astype(F32) + got.astype(F32)).astype(BF16)


def sum_over_seq(part):
    kept, sent = split_for_core(part)
    total = add_up(kept, swap(sent, 1))
    step = 2
    while step < lax.axis_size("seq"):
        total = add_up(total, swap(total, step))
        step *= 2
    return join_cores(total)


def per_device(
    hidden_in,
    frozen_query,
    key_base,
    frozen_value,
    down_query,
    query_upper_factor,
    down_value,
    value_upper_factor,
    grad_output,
):
    rows = hidden_in.shape[0]
    rank = down_query.shape[1]
    width_here = hidden_in.shape[1]
    kv_width = key_base.shape[1]
    blocks = GROUP // rows
    assert blocks == 8 and rows % 32 == 0
    routes = Routes(blocks)
    given = gather_blocks(routes, jnp.concatenate((key_base, frozen_value), axis=1))
    down = jnp.concatenate((down_query, down_value), axis=1)
    part_t = lax.dot_general(down, hidden_in, (((0,), (1,)), ((), ())), preferred_element_type=F32)
    low_t = sum_over_tensor(part_t).astype(BF16)
    low_q_t = low_t[:rank]
    low_v = gather_low(routes, low_t[rank:])

    attention, grad_up_q, back_q, back_v, back_v_sibling, grad_up_v = attention_call(
        frozen_query,
        low_q_t,
        query_upper_factor,
        value_upper_factor,
        grad_output,
        low_v,
        given,
    )

    grad_up = sum_over_seq(jnp.concatenate((grad_up_q, grad_up_v), axis=1)).astype(F32)
    back_v = (back_v + routes.core(back_v_sibling)).reshape(rank, 4, rows)
    back_v = back_v[:, 0::2] + routes.across_y(back_v[:, 1::2])
    back_v = back_v[:, 0] + routes.down(back_v[:, 1])
    back = sum_over_tensor(jnp.concatenate((back_q, back_v), axis=0)).astype(BF16)
    grad_down = dot(back, hidden_in, NN).astype(BF16)
    grad_down = sum_over_seq(jnp.concatenate((grad_down[:rank], grad_down[rank:]), axis=1))
    grad_down = grad_down.astype(F32)
    return (
        attention,
        grad_down[:, :width_here].T,
        grad_up[:, :-kv_width],
        grad_down[:, width_here:].T,
        grad_up[:, -kv_width:],
    )


def solution(mesh):
    placed = (
        P("seq", "tensor"),
        P("seq", "tensor"),
        P("seq", "tensor"),
        P("seq", "tensor"),
        P("tensor", None),
        P(None, "tensor"),
        P("tensor", None),
        P(None, "tensor"),
        P("seq", "tensor"),
    )
    return jax.shard_map(
        per_device,
        mesh=mesh,
        in_specs=placed,
        out_specs=(
            P("seq", "tensor"),
            P("tensor", None),
            P(None, "tensor"),
            P("tensor", None),
            P(None, "tensor"),
        ),
        check_vma=False,
    )
```

```python
import functools

import jax
import jax.numpy as jnp
from jax import lax
from jax.experimental import pallas as pl
from jax.experimental.pallas import tpu as pltpu
from jax.sharding import PartitionSpec as P

HD = 128
GROUP = 2048
ADAPTER_SCALE = 0.5
LOG2E = 1.4426950408889634
MASKED = -1e30
VMEM_LIMIT = 40

F32 = jnp.float32
BF16 = jnp.bfloat16
NN = (((1,), (0,)), ((), ()))
NT = (((1,), (1,)), ((), ()))

AXES = ("seq", "tensor")


def dot(a, b, dims):
    return lax.dot_general(a, b, dims, preferred_element_type=F32)


def place_in_group(blocks):
    shifted = lax.axis_index("tensor") >= lax.axis_size("tensor") // 2
    return (lax.axis_index("seq") + jnp.where(shifted, blocks // 2, 0)) % blocks


ONES = 16


def attention_body(rows, per_head, kv, stacked, blocks_in_group, *refs):
    frozen, low_q_t, up_q, up_v, grad_out = refs[:5]
    low_v = refs[5:9]
    given = refs[9:19]
    out, grad_up_q, back_q, back_v, back_v_sibling, grad_up_v = refs[19:25]
    low_q, scores, probs, grad_s, keys, keys_t, values, values_t, grad_v = refs[25:]
    scale = float(HD) ** -0.5
    to_log2 = scale * LOG2E
    place = place_in_group(blocks_in_group)
    core, y_bit, z_bit = place % 2, place // (blocks_in_group // 4) % 2, place // (blocks_in_group // 2)
    half = rows // 2
    parts = [(given[j], 0, rows) for j in range(6)]
    parts = [[p] for p in parts]
    parts += [[(given[6], 0, half), (given[7], half, half)], [(given[8], 0, half), (given[9], half, half)]]
    width_kv = kv * HD
    columns = stacked * rows
    steps = kv * per_head // stacked
    steps_per_kv = per_head // stacked
    back_q[...] = jnp.zeros_like(back_q)
    back_v[...] = jnp.zeros_like(back_v)
    back_v_sibling[...] = jnp.zeros_like(back_v)
    low_q[...] = low_q_t[...].T
    key_at = lax.broadcasted_iota(jnp.int32, (rows, columns), 0)
    query_at = lax.broadcasted_iota(jnp.int32, (rows, columns), 1) % rows

    def prepare(blocks):
        for slot, j in enumerate(blocks):
            for ref, first, count in parts[j]:
                at = slice(slot * rows + first, slot * rows + first + count)
                low_at = slice(j % 2 * rows + first, j % 2 * rows + first + count)
                block = ref[:, :width_kv]
                keys[at, :] = block
                keys_t[:, at] = block.T
                added = lax.dot_general(
                    low_v[j // 2][:, low_at], up_v[...], (((0,), (0,)), ((), ())), preferred_element_type=F32
                )
                block = (ref[:, width_kv:].astype(F32) + ADAPTER_SCALE * added).astype(BF16)
                values[at, :] = block
                block_t = block.T
                for g in range(kv):
                    values_t[g, :HD, at] = block_t[g * HD : (g + 1) * HD]
                    values_t[g, HD:, at] = jnp.ones((ONES, count), BF16)
                grad_v[at, :] = jnp.zeros((count, width_kv), F32)

    def finish(blocks):
        length = len(blocks) * rows
        rounded = grad_v[:length, :].astype(BF16)
        back = ADAPTER_SCALE * dot(up_v[...], rounded, NT)
        for slot, j in enumerate(blocks):
            target = back_v_sibling if j % 2 else back_v
            target[:, j // 2 * rows : (j // 2 + 1) * rows] = back[:, slot * rows : (slot + 1) * rows]
        low = jnp.concatenate([low_v[j // 2][...] for j in blocks[::2]], axis=1)
        grad_up_v[...] = (ADAPTER_SCALE * dot(low, rounded, NN)).astype(BF16)

    def attend(length):
        def wide(i):
            return pl.ds(pl.multiple_of(i * (stacked * HD), stacked * HD), stacked * HD)

        def narrow(i, a):
            return pl.ds(pl.multiple_of(i * (stacked * HD) + a * HD, HD), HD)

        def kv_cols(i):
            return pl.ds(pl.multiple_of((i // steps_per_kv) * HD, HD), HD)

        def score(i):
            query = frozen[:, wide(i)].astype(F32) + ADAPTER_SCALE * dot(low_q[...], up_q[:, wide(i)], NN)
            query = query.astype(BF16)
            query = jnp.concatenate([query[:, a * HD : (a + 1) * HD] for a in range(stacked)], axis=0)
            s = dot(keys[:length, kv_cols(i)], query, NT)
            own = jnp.where(key_at <= query_at, s[:rows], MASKED)
            sibling = jnp.where(core > 0, s[rows : 2 * rows], MASKED)
            scores[:rows, :] = own
            scores[rows : 2 * rows, :] = sibling
            top = jnp.max(jnp.maximum(own, sibling), axis=0, keepdims=True)
            if length > 2 * rows:
                rest = s[2 * rows :]
                scores[2 * rows : length, :] = rest
                top = jnp.maximum(top, jnp.max(rest, axis=0, keepdims=True))
            return top * to_log2

        def one_step(i, top, last=False):
            probs[:length, :] = jnp.exp2(scores[:length, :] * to_log2 - top).astype(BF16)
            later = top if last else score(i + 1)
            attended = dot(values_t[i // steps_per_kv, :, :length], probs[:length, :], NN)
            inverse = 1.0 / attended[HD : HD + 1, :]
            attended = (attended[:HD] * inverse).astype(BF16)
            for a in range(stacked):
                out[:, narrow(i, a)] = attended[:, a * rows : (a + 1) * rows].T
            upstream = jnp.concatenate([grad_out[:, narrow(i, a)].T for a in range(stacked)], axis=1)
            upstream_f = upstream.astype(F32)
            delta = jnp.sum(upstream_f * attended.astype(F32), axis=0, keepdims=True)
            normed = (upstream_f * inverse).astype(BF16)
            grad_probs = dot(values[:length, kv_cols(i)], upstream, NN)
            grad_s[:length, :] = (probs[:length, :].astype(F32) * (grad_probs - delta)).astype(BF16)
            grad_v[:length, kv_cols(i)] += dot(probs[:length, :], normed, NT)
            grad_query = dot(keys_t[kv_cols(i), :length], grad_s[:length, :], NN)
            grad_query = (grad_query * (inverse * scale)).astype(BF16)
            back = None
            for a in range(stacked):
                one = grad_query[:, a * rows : (a + 1) * rows]
                grad_up_q[:, narrow(i, a)] = (ADAPTER_SCALE * dot(low_q_t[...], one, NT)).astype(BF16)
                term = dot(up_q[:, narrow(i, a)], one, NN)
                back = term if back is None else back + term
            back_q[...] += ADAPTER_SCALE * back

            return later

        top = lax.fori_loop(0, steps - 1, one_step, score(0))
        one_step(jnp.int32(steps - 1), top, last=True)

    for y in (0, 1):
        for z in (0, 1):

            @pl.when((y_bit == y) & (z_bit == z))
            def _():
                blocks = [0, 1] + [2, 3] * y + [4, 5, 6, 7] * z
                prepare(blocks)
                attend(len(blocks) * rows)
                finish(blocks)


def attention_call(frozen, low_q_t, up_q, up_v, grad_out, low_v, given):
    rows, width = frozen.shape
    kv = up_v.shape[1] // HD
    rank = up_q.shape[0]
    per_head = width // HD // kv
    reach = GROUP
    stacked = 2
    vmem = pl.BlockSpec(memory_space=pltpu.VMEM)
    pairs = rows * reach * per_head * kv
    return pl.pallas_call(
        functools.partial(attention_body, rows, per_head, kv, stacked, GROUP // rows),
        in_specs=[vmem] * (5 + len(low_v) + len(given)),
        out_specs=[vmem] * 6,
        scratch_shapes=[
            pltpu.VMEM((rows, rank), BF16),
            pltpu.VMEM((reach, stacked * rows), F32),
            pltpu.VMEM((reach, stacked * rows), BF16),
            pltpu.VMEM((reach, stacked * rows), BF16),
            pltpu.VMEM((reach, kv * HD), BF16),
            pltpu.VMEM((kv * HD, reach), BF16),
            pltpu.VMEM((reach, kv * HD), BF16),
            pltpu.VMEM((kv, HD + ONES, reach), BF16),
            pltpu.VMEM((reach, kv * HD), F32),
        ],
        out_shape=[
            jax.ShapeDtypeStruct((rows, width), BF16),
            jax.ShapeDtypeStruct((rank, width), BF16),
            jax.ShapeDtypeStruct((rank, rows), F32),
            jax.ShapeDtypeStruct((rank, reach // 2), F32),
            jax.ShapeDtypeStruct((rank, reach // 2), F32),
            jax.ShapeDtypeStruct((rank, kv * HD), BF16),
        ],
        compiler_params=pltpu.CompilerParams(vmem_limit_bytes=VMEM_LIMIT * 2**20),
        cost_estimate=pl.CostEstimate(
            flops=10 * pairs * HD, bytes_accessed=16 * rows * width, transcendentals=pairs
        ),
    )(frozen, low_q_t, up_q, up_v, grad_out, *low_v, *given)


class Routes:
    def __init__(self, blocks):
        self.seq = lax.axis_size("seq")
        self.tensor = lax.axis_size("tensor")
        self.half = blocks // 2
        self.y = blocks // 4

    def upper(self, s, t):
        offset = self.half if t >= self.tensor // 2 else 0
        return ((s - offset) // self.half) % 2 == 1

    def send(self, block, target):
        route = []
        for s in range(self.seq):
            for t in range(self.tensor):
                to = target(s, t)
                if to is not None:
                    route.append((s * self.tensor + t, to % self.seq * self.tensor + t))
        return lax.ppermute(block, AXES, route)

    def core(self, block):
        return self.send(block, lambda s, t: s ^ 1)

    def across_y(self, block):
        return self.send(block, lambda s, t: s ^ self.y)

    def own_across_y(self, block):
        return self.send(
            block, lambda s, t: None if self.upper(s, t) and s & self.y else s ^ self.y
        )

    def up(self, block):
        return self.send(block, lambda s, t: None if self.upper(s, t) else s + self.half)

    def up_across_y(self, block):
        return self.send(
            block, lambda s, t: None if self.upper(s, t) else (s + self.half) ^ self.y
        )

    def within_upper(self, block):
        return self.send(block, lambda s, t: s ^ self.y if self.upper(s, t) else None)

    def down(self, block):
        return self.send(block, lambda s, t: s - self.half if self.upper(s, t) else None)


def gather_blocks(routes, own):
    cut = own.shape[0] // 2
    from_y = routes.own_across_y(own)
    from_z = routes.up(own)
    first = routes.up(from_y[:cut])
    second = routes.within_upper(from_z[cut:])
    found = []
    for block in (own, from_y, from_z):
        found += [block, routes.core(block)]
    return found + [first, second, routes.core(first), routes.core(second)]


def gather_low(routes, own):
    both = jnp.concatenate((own, routes.core(own)), axis=1)
    return [both, routes.across_y(both), routes.up(both), routes.up_across_y(both)]


def sum_over_tensor(part):
    size = lax.axis_size("tensor")
    step = 1
    while step < size:
        part = part + lax.ppermute(part, "tensor", [(i, i ^ step) for i in range(size)])
        step *= 2
    return part


def swap(block, step):
    return lax.ppermute(block, "seq", [(i, i ^ step) for i in range(lax.axis_size("seq"))])


def split_for_core(part):
    odd = lax.axis_index("seq") % 2 == 1
    half = part.shape[1] // 2
    low, high = part[:, :half], part[:, half:]
    return jnp.where(odd, high, low), jnp.where(odd, low, high)


def join_cores(total):
    odd = lax.axis_index("seq") % 2 == 1
    got = swap(total, 1)
    return jnp.concatenate((jnp.where(odd, got, total), jnp.where(odd, total, got)), axis=1)


def add_up(mine, got):
    return (mine.astype(F32) + got.astype(F32)).astype(BF16)


def sum_over_chips(total, step):
    while step < lax.axis_size("seq"):
        total = add_up(total, swap(total, step))
        step *= 2
    return total


def per_device(
    hidden_in,
    frozen_query,
    key_base,
    frozen_value,
    down_query,
    query_upper_factor,
    down_value,
    value_upper_factor,
    grad_output,
):
    rows = hidden_in.shape[0]
    rank = down_query.shape[1]
    width_here = hidden_in.shape[1]
    kv_width = key_base.shape[1]
    blocks = GROUP // rows
    assert blocks == 8 and rows % 32 == 0
    routes = Routes(blocks)
    given = gather_blocks(routes, jnp.concatenate((key_base, frozen_value), axis=1))
    down = jnp.concatenate((down_query, down_value), axis=1)
    part_t = lax.dot_general(down, hidden_in, (((0,), (1,)), ((), ())), preferred_element_type=F32)
    low_t = sum_over_tensor(part_t).astype(BF16)
    low_q_t = low_t[:rank]
    low_v = gather_low(routes, low_t[rank:])

    attention, grad_up_q, back_q, back_v, back_v_sibling, grad_up_v = attention_call(
        frozen_query,
        low_q_t,
        query_upper_factor,
        value_upper_factor,
        grad_output,
        low_v,
        given,
    )

    back_v = (back_v + routes.core(back_v_sibling)).reshape(rank, 4, rows)
    back_v = back_v[:, 0::2] + routes.across_y(back_v[:, 1::2])
    back_v = back_v[:, 0] + routes.down(back_v[:, 1])
    back = sum_over_tensor(jnp.concatenate((back_q, back_v), axis=0)).astype(BF16)
    grad_down = dot(back, hidden_in, NN).astype(BF16)
    odd = lax.axis_index("seq") % 2 == 1
    of_query, of_value = grad_down[:rank], grad_down[rank:]
    total = add_up(jnp.where(odd, of_value, of_query), swap(jnp.where(odd, of_query, of_value), 1))
    kept, sent = split_for_core(jnp.concatenate((grad_up_q, grad_up_v), axis=1))
    grad_up = sum_over_chips(add_up(kept, swap(sent, 1)), 2)
    total, grad_up = lax.optimization_barrier((add_up(total, swap(total, 2)), grad_up))
    total = sum_over_chips(total, 4)
    grad_up = join_cores(grad_up).astype(F32)
    got = swap(total, 1)
    return (
        attention,
        jnp.where(odd, got, total).astype(F32).T,
        grad_up[:, :-kv_width],
        jnp.where(odd, total, got).astype(F32).T,
        grad_up[:, -kv_width:],
    )


def solution(mesh):
    placed = (
        P("seq", "tensor"),
        P("seq", "tensor"),
        P("seq", "tensor"),
        P("seq", "tensor"),
        P("tensor", None),
        P(None, "tensor"),
        P("tensor", None),
        P(None, "tensor"),
        P("seq", "tensor"),
    )
    return jax.shard_map(
        per_device,
        mesh=mesh,
        in_specs=placed,
        out_specs=(
            P("seq", "tensor"),
            P("tensor", None),
            P(None, "tensor"),
            P("tensor", None),
            P(None, "tensor"),
        ),
        check_vma=False,
    )
```

```python
import functools

import jax
import jax.numpy as jnp
from jax import lax
from jax.experimental import pallas as pl
from jax.experimental.pallas import tpu as pltpu
from jax.sharding import PartitionSpec as P

HD = 128
GROUP = 2048
ADAPTER_SCALE = 0.5
LOG2E = 1.4426950408889634
MASKED = -1e30
VMEM_LIMIT = 40

F32 = jnp.float32
BF16 = jnp.bfloat16
NN = (((1,), (0,)), ((), ()))
NT = (((1,), (1,)), ((), ()))

AXES = ("seq", "tensor")


def dot(a, b, dims):
    return lax.dot_general(a, b, dims, preferred_element_type=F32)


def place_in_group(blocks):
    shifted = lax.axis_index("tensor") >= lax.axis_size("tensor") // 2
    return (lax.axis_index("seq") + jnp.where(shifted, blocks // 2, 0)) % blocks


ONES = 16


def attention_body(rows, per_head, kv, stacked, blocks_in_group, *refs):
    queries, low_q_t, up_q, up_v, grad_out = refs[:5]
    low_v = refs[5:9]
    given = refs[9:19]
    out, grad_up_q, back_q, back_v, back_v_sibling, grad_up_v = refs[19:25]
    scores, probs, grad_s, keys, keys_t, values, values_t, grad_v, grad_q = refs[25:]
    scale = float(HD) ** -0.5
    to_log2 = scale * LOG2E
    place = place_in_group(blocks_in_group)
    core, y_bit, z_bit = place % 2, place // (blocks_in_group // 4) % 2, place // (blocks_in_group // 2)
    half = rows // 2
    parts = [(given[j], 0, rows) for j in range(6)]
    parts = [[p] for p in parts]
    parts += [[(given[6], 0, half), (given[7], half, half)], [(given[8], 0, half), (given[9], half, half)]]
    width_kv = kv * HD
    columns = stacked * rows
    steps = kv * per_head // stacked
    steps_per_kv = per_head // stacked
    back_v[...] = jnp.zeros_like(back_v)
    back_v_sibling[...] = jnp.zeros_like(back_v)
    key_at = lax.broadcasted_iota(jnp.int32, (rows, columns), 0)
    query_at = lax.broadcasted_iota(jnp.int32, (rows, columns), 1) % rows

    def prepare(blocks):
        for slot, j in enumerate(blocks):
            for ref, first, count in parts[j]:
                at = slice(slot * rows + first, slot * rows + first + count)
                low_at = slice(j % 2 * rows + first, j % 2 * rows + first + count)
                block = ref[:, :width_kv]
                keys[at, :] = block
                keys_t[:, at] = block.T
                added = lax.dot_general(
                    low_v[j // 2][:, low_at], up_v[...], (((0,), (0,)), ((), ())), preferred_element_type=F32
                )
                block = (ref[:, width_kv:].astype(F32) + ADAPTER_SCALE * added).astype(BF16)
                values[at, :] = block
                block_t = block.T
                for g in range(kv):
                    values_t[g, :HD, at] = block_t[g * HD : (g + 1) * HD]
                    values_t[g, HD:, at] = jnp.ones((ONES, count), BF16)
                grad_v[at, :] = jnp.zeros((count, width_kv), F32)

    def finish(blocks):
        grad_up_q[...] = (ADAPTER_SCALE * dot(low_q_t[...], grad_q[...], NT)).astype(BF16)
        back_q[...] = ADAPTER_SCALE * dot(up_q[...], grad_q[...], NN)
        length = len(blocks) * rows
        rounded = grad_v[:length, :].astype(BF16)
        back = ADAPTER_SCALE * dot(up_v[...], rounded, NT)
        for slot, j in enumerate(blocks):
            target = back_v_sibling if j % 2 else back_v
            target[:, j // 2 * rows : (j // 2 + 1) * rows] = back[:, slot * rows : (slot + 1) * rows]
        low = jnp.concatenate([low_v[j // 2][...] for j in blocks[::2]], axis=1)
        grad_up_v[...] = (ADAPTER_SCALE * dot(low, rounded, NN)).astype(BF16)

    def attend(length):
        def wide(i):
            return pl.ds(pl.multiple_of(i * (stacked * HD), stacked * HD), stacked * HD)

        def narrow(i, a):
            return pl.ds(pl.multiple_of(i * (stacked * HD) + a * HD, HD), HD)

        def kv_cols(i):
            return pl.ds(pl.multiple_of((i // steps_per_kv) * HD, HD), HD)

        def score(i):
            query = queries[:, wide(i)]
            query = jnp.concatenate([query[:, a * HD : (a + 1) * HD] for a in range(stacked)], axis=0)
            s = dot(keys[:length, kv_cols(i)], query, NT)
            own = jnp.where(key_at <= query_at, s[:rows], MASKED)
            sibling = jnp.where(core > 0, s[rows : 2 * rows], MASKED)
            scores[:rows, :] = own
            scores[rows : 2 * rows, :] = sibling
            top = jnp.max(jnp.maximum(own, sibling), axis=0, keepdims=True)
            if length > 2 * rows:
                rest = s[2 * rows :]
                scores[2 * rows : length, :] = rest
                top = jnp.maximum(top, jnp.max(rest, axis=0, keepdims=True))
            return top * to_log2

        def one_step(i, top, last=False):
            probs[:length, :] = jnp.exp2(scores[:length, :] * to_log2 - top).astype(BF16)
            later = top if last else score(i + 1)
            attended = dot(values_t[i // steps_per_kv, :, :length], probs[:length, :], NN)
            inverse = 1.0 / attended[HD : HD + 1, :]
            attended = (attended[:HD] * inverse).astype(BF16)
            for a in range(stacked):
                out[:, narrow(i, a)] = attended[:, a * rows : (a + 1) * rows].T
            upstream = jnp.concatenate([grad_out[:, narrow(i, a)].T for a in range(stacked)], axis=1)
            upstream_f = upstream.astype(F32)
            delta = jnp.sum(upstream_f * attended.astype(F32), axis=0, keepdims=True)
            normed = (upstream_f * inverse).astype(BF16)
            grad_probs = dot(values[:length, kv_cols(i)], upstream, NN)
            grad_s[:length, :] = (probs[:length, :].astype(F32) * (grad_probs - delta)).astype(BF16)
            grad_v[:length, kv_cols(i)] += dot(probs[:length, :], normed, NT)
            grad_query = dot(keys_t[kv_cols(i), :length], grad_s[:length, :], NN)
            grad_query = (grad_query * (inverse * scale)).astype(BF16)
            for a in range(stacked):
                grad_q[narrow(i, a), :] = grad_query[:, a * rows : (a + 1) * rows]
            return later

        top = lax.fori_loop(0, steps - 1, one_step, score(0))
        one_step(jnp.int32(steps - 1), top, last=True)

    for y in (0, 1):
        for z in (0, 1):

            @pl.when((y_bit == y) & (z_bit == z))
            def _():
                blocks = [0, 1] + [2, 3] * y + [4, 5, 6, 7] * z
                prepare(blocks)
                attend(len(blocks) * rows)
                finish(blocks)


def attention_call(queries, low_q_t, up_q, up_v, grad_out, low_v, given):
    rows, width = queries.shape
    kv = up_v.shape[1] // HD
    rank = up_q.shape[0]
    per_head = width // HD // kv
    reach = GROUP
    stacked = 2
    vmem = pl.BlockSpec(memory_space=pltpu.VMEM)
    pairs = rows * reach * per_head * kv
    return pl.pallas_call(
        functools.partial(attention_body, rows, per_head, kv, stacked, GROUP // rows),
        in_specs=[vmem] * (5 + len(low_v) + len(given)),
        out_specs=[vmem] * 6,
        scratch_shapes=[
            pltpu.VMEM((reach, stacked * rows), F32),
            pltpu.VMEM((reach, stacked * rows), BF16),
            pltpu.VMEM((reach, stacked * rows), BF16),
            pltpu.VMEM((reach, kv * HD), BF16),
            pltpu.VMEM((kv * HD, reach), BF16),
            pltpu.VMEM((reach, kv * HD), BF16),
            pltpu.VMEM((kv, HD + ONES, reach), BF16),
            pltpu.VMEM((reach, kv * HD), F32),
            pltpu.VMEM((width, rows), BF16),
        ],
        out_shape=[
            jax.ShapeDtypeStruct((rows, width), BF16),
            jax.ShapeDtypeStruct((rank, width), BF16),
            jax.ShapeDtypeStruct((rank, rows), F32),
            jax.ShapeDtypeStruct((rank, reach // 2), F32),
            jax.ShapeDtypeStruct((rank, reach // 2), F32),
            jax.ShapeDtypeStruct((rank, kv * HD), BF16),
        ],
        compiler_params=pltpu.CompilerParams(vmem_limit_bytes=VMEM_LIMIT * 2**20),
        cost_estimate=pl.CostEstimate(
            flops=10 * pairs * HD, bytes_accessed=16 * rows * width, transcendentals=pairs
        ),
    )(queries, low_q_t, up_q, up_v, grad_out, *low_v, *given)


class Routes:
    def __init__(self, blocks):
        self.seq = lax.axis_size("seq")
        self.tensor = lax.axis_size("tensor")
        self.half = blocks // 2
        self.y = blocks // 4

    def upper(self, s, t):
        offset = self.half if t >= self.tensor // 2 else 0
        return ((s - offset) // self.half) % 2 == 1

    def send(self, block, target):
        route = []
        for s in range(self.seq):
            for t in range(self.tensor):
                to = target(s, t)
                if to is not None:
                    route.append((s * self.tensor + t, to % self.seq * self.tensor + t))
        return lax.ppermute(block, AXES, route)

    def core(self, block):
        return self.send(block, lambda s, t: s ^ 1)

    def across_y(self, block):
        return self.send(block, lambda s, t: s ^ self.y)

    def own_across_y(self, block):
        return self.send(
            block, lambda s, t: None if self.upper(s, t) and s & self.y else s ^ self.y
        )

    def up(self, block):
        return self.send(block, lambda s, t: None if self.upper(s, t) else s + self.half)

    def up_across_y(self, block):
        return self.send(
            block, lambda s, t: None if self.upper(s, t) else (s + self.half) ^ self.y
        )

    def within_upper(self, block):
        return self.send(block, lambda s, t: s ^ self.y if self.upper(s, t) else None)

    def down(self, block):
        return self.send(block, lambda s, t: s - self.half if self.upper(s, t) else None)


def gather_near(routes, own):
    return routes.own_across_y(own), routes.up(own)


def gather_far(routes, own, from_y, from_z):
    cut = own.shape[0] // 2
    first = routes.up(from_y[:cut])
    second = routes.within_upper(from_z[cut:])
    found = []
    for block in (own, from_y, from_z):
        found += [block, routes.core(block)]
    return found + [first, second, routes.core(first), routes.core(second)]


def gather_low(routes, own):
    both = jnp.concatenate((own, routes.core(own)), axis=1)
    return [both, routes.across_y(both), routes.up(both), routes.up_across_y(both)]


def sum_over_tensor(part):
    size = lax.axis_size("tensor")
    step = 1
    while step < size:
        part = part + lax.ppermute(part, "tensor", [(i, i ^ step) for i in range(size)])
        step *= 2
    return part


def swap(block, step):
    return lax.ppermute(block, "seq", [(i, i ^ step) for i in range(lax.axis_size("seq"))])


def split_for_core(part):
    odd = lax.axis_index("seq") % 2 == 1
    half = part.shape[1] // 2
    low, high = part[:, :half], part[:, half:]
    return jnp.where(odd, high, low), jnp.where(odd, low, high)


def join_cores(total):
    odd = lax.axis_index("seq") % 2 == 1
    got = swap(total, 1)
    return jnp.concatenate((jnp.where(odd, got, total), jnp.where(odd, total, got)), axis=1)


def add_up(mine, got):
    return (mine.astype(F32) + got.astype(F32)).astype(BF16)


def sum_over_chips(total, step):
    while step < lax.axis_size("seq"):
        total = add_up(total, swap(total, step))
        step *= 2
    return total


def per_device(
    hidden_in,
    frozen_query,
    key_base,
    frozen_value,
    down_query,
    query_upper_factor,
    down_value,
    value_upper_factor,
    grad_output,
):
    rows = hidden_in.shape[0]
    rank = down_query.shape[1]
    width_here = hidden_in.shape[1]
    kv_width = key_base.shape[1]
    blocks = GROUP // rows
    assert blocks == 8 and rows % 32 == 0
    routes = Routes(blocks)
    own = jnp.concatenate((key_base, frozen_value), axis=1)
    near = gather_near(routes, own)
    down = jnp.concatenate((down_query, down_value), axis=1)
    part_t = lax.dot_general(down, hidden_in, (((0,), (1,)), ((), ())), preferred_element_type=F32)
    low_t = sum_over_tensor(part_t).astype(BF16)
    low_q_t = low_t[:rank]
    low_v = gather_low(routes, low_t[rank:])
    near, low_v = lax.optimization_barrier((near, low_v))
    given = gather_far(routes, own, *near)
    queries = (
        frozen_query.astype(F32)
        + ADAPTER_SCALE
        * lax.dot_general(
            low_q_t, query_upper_factor, (((0,), (0,)), ((), ())), preferred_element_type=F32
        )
    ).astype(BF16)

    attention, grad_up_q, back_q, back_v, back_v_sibling, grad_up_v = attention_call(
        queries,
        low_q_t,
        query_upper_factor,
        value_upper_factor,
        grad_output,
        low_v,
        given,
    )

    back_v = (back_v + routes.core(back_v_sibling)).reshape(rank, 4, rows)
    back_v = back_v[:, 0::2] + routes.across_y(back_v[:, 1::2])
    back_v = back_v[:, 0] + routes.down(back_v[:, 1])
    back = sum_over_tensor(jnp.concatenate((back_q, back_v), axis=0)).astype(BF16)
    grad_down = dot(back, hidden_in, NN).astype(BF16)
    odd = lax.axis_index("seq") % 2 == 1
    of_query, of_value = grad_down[:rank], grad_down[rank:]
    total = add_up(jnp.where(odd, of_value, of_query), swap(jnp.where(odd, of_query, of_value), 1))
    kept, sent = split_for_core(jnp.concatenate((grad_up_q, grad_up_v), axis=1))
    grad_up = sum_over_chips(add_up(kept, swap(sent, 1)), 2)
    total, grad_up = lax.optimization_barrier((add_up(total, swap(total, 2)), grad_up))
    total = sum_over_chips(total, 4)
    grad_up = join_cores(grad_up).astype(F32)
    got = swap(total, 1)
    return (
        attention,
        jnp.where(odd, got, total).astype(F32).T,
        grad_up[:, :-kv_width],
        jnp.where(odd, total, got).astype(F32).T,
        grad_up[:, -kv_width:],
    )


def solution(mesh):
    placed = (
        P("seq", "tensor"),
        P("seq", "tensor"),
        P("seq", "tensor"),
        P("seq", "tensor"),
        P("tensor", None),
        P(None, "tensor"),
        P("tensor", None),
        P(None, "tensor"),
        P("seq", "tensor"),
    )
    return jax.shard_map(
        per_device,
        mesh=mesh,
        in_specs=placed,
        out_specs=(
            P("seq", "tensor"),
            P("tensor", None),
            P(None, "tensor"),
            P("tensor", None),
            P(None, "tensor"),
        ),
        check_vma=False,
    )
```

```python
import functools

import jax
import jax.numpy as jnp
from jax import lax
from jax.experimental import pallas as pl
from jax.experimental.pallas import tpu as pltpu
from jax.sharding import PartitionSpec as P

HD = 128
GROUP = 2048
ADAPTER_SCALE = 0.5
LOG2E = 1.4426950408889634
MASKED = -1e30
VMEM_LIMIT = 40

F32 = jnp.float32
BF16 = jnp.bfloat16
NN = (((1,), (0,)), ((), ()))
NT = (((1,), (1,)), ((), ()))

AXES = ("seq", "tensor")


def dot(a, b, dims):
    return lax.dot_general(a, b, dims, preferred_element_type=F32)


def place_in_group(blocks):
    shifted = lax.axis_index("tensor") >= lax.axis_size("tensor") // 2
    return (lax.axis_index("seq") + jnp.where(shifted, blocks // 2, 0)) % blocks


ONES = 16


def attention_body(rows, per_head, kv, stacked, blocks_in_group, *refs):
    queries, low_q_t, up_q, up_v, grad_out = refs[:5]
    low_v = refs[5:9]
    given = refs[9:19]
    out, grad_up_q, back_q, back_v, back_v_sibling, grad_up_v = refs[19:25]
    scores, probs, grad_s, keys, keys_t, values, values_t, grad_v, grad_q = refs[25:]
    scale = float(HD) ** -0.5
    to_log2 = scale * LOG2E
    place = place_in_group(blocks_in_group)
    core, y_bit, z_bit = place % 2, place // (blocks_in_group // 4) % 2, place // (blocks_in_group // 2)
    half = rows // 2
    parts = [(given[j], 0, rows) for j in range(6)]
    parts = [[p] for p in parts]
    parts += [[(given[6], 0, half), (given[7], half, half)], [(given[8], 0, half), (given[9], half, half)]]
    width_kv = kv * HD
    columns = stacked * rows
    steps = kv * per_head // stacked
    steps_per_kv = per_head // stacked
    back_v[...] = jnp.zeros_like(back_v)
    back_v_sibling[...] = jnp.zeros_like(back_v)
    key_at = lax.broadcasted_iota(jnp.int32, (rows, columns), 0)
    query_at = lax.broadcasted_iota(jnp.int32, (rows, columns), 1) % rows

    def prepare(blocks):
        for slot, j in enumerate(blocks):
            for ref, first, count in parts[j]:
                at = slice(slot * rows + first, slot * rows + first + count)
                low_at = slice(j % 2 * rows + first, j % 2 * rows + first + count)
                block = ref[:, :width_kv]
                keys[at, :] = block
                keys_t[:, at] = block.T
                added = lax.dot_general(
                    low_v[j // 2][:, low_at], up_v[...], (((0,), (0,)), ((), ())), preferred_element_type=F32
                )
                block = (ref[:, width_kv:].astype(F32) + ADAPTER_SCALE * added).astype(BF16)
                values[at, :] = block
                block_t = block.T
                for g in range(kv):
                    values_t[g, :HD, at] = block_t[g * HD : (g + 1) * HD]
                    values_t[g, HD:, at] = jnp.ones((ONES, count), BF16)
                grad_v[at, :] = jnp.zeros((count, width_kv), F32)

    def finish(blocks):
        grad_up_q[...] = (ADAPTER_SCALE * dot(low_q_t[...], grad_q[...], NT)).astype(BF16)
        back_q[...] = ADAPTER_SCALE * dot(up_q[...], grad_q[...], NN)
        length = len(blocks) * rows
        rounded = grad_v[:length, :].astype(BF16)
        back = ADAPTER_SCALE * dot(up_v[...], rounded, NT)
        for slot, j in enumerate(blocks):
            target = back_v_sibling if j % 2 else back_v
            target[:, j // 2 * rows : (j // 2 + 1) * rows] = back[:, slot * rows : (slot + 1) * rows]
        low = jnp.concatenate([low_v[j // 2][...] for j in blocks[::2]], axis=1)
        grad_up_v[...] = (ADAPTER_SCALE * dot(low, rounded, NN)).astype(BF16)

    def attend(length):
        def wide(i):
            return pl.ds(pl.multiple_of(i * (stacked * HD), stacked * HD), stacked * HD)

        def narrow(i, a):
            return pl.ds(pl.multiple_of(i * (stacked * HD) + a * HD, HD), HD)

        def kv_cols(i):
            return pl.ds(pl.multiple_of((i // steps_per_kv) * HD, HD), HD)

        def score(i):
            query = queries[:, wide(i)]
            query = jnp.concatenate([query[:, a * HD : (a + 1) * HD] for a in range(stacked)], axis=0)
            s = dot(keys[:length, kv_cols(i)], query, NT)
            own = jnp.where(key_at <= query_at, s[:rows], MASKED)
            sibling = jnp.where(core > 0, s[rows : 2 * rows], MASKED)
            scores[:rows, :] = own
            scores[rows : 2 * rows, :] = sibling
            top = jnp.max(jnp.maximum(own, sibling), axis=0, keepdims=True)
            if length > 2 * rows:
                rest = s[2 * rows :]
                scores[2 * rows : length, :] = rest
                top = jnp.maximum(top, jnp.max(rest, axis=0, keepdims=True))
            return top * to_log2

        def one_step(i, top, last=False):
            probs[:length, :] = jnp.exp2(scores[:length, :] * to_log2 - top).astype(BF16)
            later = top if last else score(i + 1)
            attended = dot(values_t[i // steps_per_kv, :, :length], probs[:length, :], NN)
            inverse = 1.0 / attended[HD : HD + 1, :]
            attended = (attended[:HD] * inverse).astype(BF16)
            for a in range(stacked):
                out[:, narrow(i, a)] = attended[:, a * rows : (a + 1) * rows].T
            upstream = jnp.concatenate([grad_out[:, narrow(i, a)].T for a in range(stacked)], axis=1)
            upstream_f = upstream.astype(F32)
            delta = jnp.sum(upstream_f * attended.astype(F32), axis=0, keepdims=True)
            normed = (upstream_f * inverse).astype(BF16)
            grad_probs = dot(values[:length, kv_cols(i)], upstream, NN)
            grad_s[:length, :] = (probs[:length, :].astype(F32) * (grad_probs - delta)).astype(BF16)
            grad_v[:length, kv_cols(i)] += dot(probs[:length, :], normed, NT)
            grad_query = dot(keys_t[kv_cols(i), :length], grad_s[:length, :], NN)
            grad_query = (grad_query * (inverse * scale)).astype(BF16)
            for a in range(stacked):
                grad_q[narrow(i, a), :] = grad_query[:, a * rows : (a + 1) * rows]
            return later

        top = lax.fori_loop(0, steps - 1, one_step, score(0))
        one_step(jnp.int32(steps - 1), top, last=True)

    for y in (0, 1):
        for z in (0, 1):

            @pl.when((y_bit == y) & (z_bit == z))
            def _():
                blocks = [0, 1] + [2, 3] * y + [4, 5, 6, 7] * z
                prepare(blocks)
                attend(len(blocks) * rows)
                finish(blocks)


def attention_call(queries, low_q_t, up_q, up_v, grad_out, low_v, given):
    rows, width = queries.shape
    kv = up_v.shape[1] // HD
    rank = up_q.shape[0]
    per_head = width // HD // kv
    reach = GROUP
    stacked = 2
    vmem = pl.BlockSpec(memory_space=pltpu.VMEM)
    pairs = rows * reach * per_head * kv
    return pl.pallas_call(
        functools.partial(attention_body, rows, per_head, kv, stacked, GROUP // rows),
        in_specs=[vmem] * (5 + len(low_v) + len(given)),
        out_specs=[vmem] * 6,
        scratch_shapes=[
            pltpu.VMEM((reach, stacked * rows), F32),
            pltpu.VMEM((reach, stacked * rows), BF16),
            pltpu.VMEM((reach, stacked * rows), BF16),
            pltpu.VMEM((reach, kv * HD), BF16),
            pltpu.VMEM((kv * HD, reach), BF16),
            pltpu.VMEM((reach, kv * HD), BF16),
            pltpu.VMEM((kv, HD + ONES, reach), BF16),
            pltpu.VMEM((reach, kv * HD), F32),
            pltpu.VMEM((width, rows), BF16),
        ],
        out_shape=[
            jax.ShapeDtypeStruct((rows, width), BF16),
            jax.ShapeDtypeStruct((rank, width), BF16),
            jax.ShapeDtypeStruct((rank, rows), F32),
            jax.ShapeDtypeStruct((rank, reach // 2), F32),
            jax.ShapeDtypeStruct((rank, reach // 2), F32),
            jax.ShapeDtypeStruct((rank, kv * HD), BF16),
        ],
        compiler_params=pltpu.CompilerParams(vmem_limit_bytes=VMEM_LIMIT * 2**20),
        cost_estimate=pl.CostEstimate(
            flops=10 * pairs * HD, bytes_accessed=16 * rows * width, transcendentals=pairs
        ),
    )(queries, low_q_t, up_q, up_v, grad_out, *low_v, *given)


class Routes:
    def __init__(self, blocks):
        self.seq = lax.axis_size("seq")
        self.tensor = lax.axis_size("tensor")
        self.half = blocks // 2
        self.y = blocks // 4

    def upper(self, s, t):
        offset = self.half if t >= self.tensor // 2 else 0
        return ((s - offset) // self.half) % 2 == 1

    def send(self, block, target):
        route = []
        for s in range(self.seq):
            for t in range(self.tensor):
                to = target(s, t)
                if to is not None:
                    route.append((s * self.tensor + t, to % self.seq * self.tensor + t))
        return lax.ppermute(block, AXES, route)

    def core(self, block):
        return self.send(block, lambda s, t: s ^ 1)

    def across_y(self, block):
        return self.send(block, lambda s, t: s ^ self.y)

    def own_across_y(self, block):
        return self.send(
            block, lambda s, t: None if self.upper(s, t) and s & self.y else s ^ self.y
        )

    def up(self, block):
        return self.send(block, lambda s, t: None if self.upper(s, t) else s + self.half)

    def up_across_y(self, block):
        return self.send(
            block, lambda s, t: None if self.upper(s, t) else (s + self.half) ^ self.y
        )

    def within_upper(self, block):
        return self.send(block, lambda s, t: s ^ self.y if self.upper(s, t) else None)

    def down(self, block):
        return self.send(block, lambda s, t: s - self.half if self.upper(s, t) else None)


def gather_near(routes, own):
    return routes.own_across_y(own), routes.up(own)


def gather_far(routes, own, from_y, from_z):
    cut = own.shape[0] // 2
    first = routes.up(from_y[:cut])
    second = routes.within_upper(from_z[cut:])
    found = []
    for block in (own, from_y, from_z):
        found += [block, routes.core(block)]
    return found + [first, second, routes.core(first), routes.core(second)]


def gather_low(routes, own):
    both = jnp.concatenate((own, routes.core(own)), axis=1)
    return [both, routes.across_y(both), routes.up(both), routes.up_across_y(both)]


def sum_over_tensor(part):
    size = lax.axis_size("tensor")
    step = 1
    while step < size:
        part = part + lax.ppermute(part, "tensor", [(i, i ^ step) for i in range(size)])
        step *= 2
    return part


def swap(block, step):
    return lax.ppermute(block, "seq", [(i, i ^ step) for i in range(lax.axis_size("seq"))])


def split_for_core(part):
    odd = lax.axis_index("seq") % 2 == 1
    half = part.shape[1] // 2
    low, high = part[:, :half], part[:, half:]
    return jnp.where(odd, high, low), jnp.where(odd, low, high)


def join_cores(total):
    odd = lax.axis_index("seq") % 2 == 1
    got = swap(total, 1)
    return jnp.concatenate((jnp.where(odd, got, total), jnp.where(odd, total, got)), axis=1)


def add_up(mine, got):
    return (mine.astype(F32) + got.astype(F32)).astype(BF16)


def sum_over_chips(total, step):
    while step < lax.axis_size("seq"):
        total = add_up(total, swap(total, step))
        step *= 2
    return total


def per_device(
    hidden_in,
    frozen_query,
    key_base,
    frozen_value,
    down_query,
    query_upper_factor,
    down_value,
    value_upper_factor,
    grad_output,
):
    rows = hidden_in.shape[0]
    rank = down_query.shape[1]
    width_here = hidden_in.shape[1]
    kv_width = key_base.shape[1]
    blocks = GROUP // rows
    assert blocks == 8 and rows % 32 == 0
    routes = Routes(blocks)
    own = jnp.concatenate((key_base, frozen_value), axis=1)
    near = gather_near(routes, own)
    down = jnp.concatenate((down_query, down_value), axis=1)
    part_t = lax.dot_general(down, hidden_in, (((0,), (1,)), ((), ())), preferred_element_type=F32)
    low_t = sum_over_tensor(part_t).astype(BF16)
    low_q_t = low_t[:rank]
    low_v = gather_low(routes, low_t[rank:])
    queries = (
        frozen_query.astype(F32)
        + ADAPTER_SCALE
        * lax.dot_general(
            low_q_t, query_upper_factor, (((0,), (0,)), ((), ())), preferred_element_type=F32
        )
    ).astype(BF16)
    near, low_v, queries = lax.optimization_barrier((near, low_v, queries))
    given = gather_far(routes, own, *near)

    attention, grad_up_q, back_q, back_v, back_v_sibling, grad_up_v = attention_call(
        queries,
        low_q_t,
        query_upper_factor,
        value_upper_factor,
        grad_output,
        low_v,
        given,
    )

    back_v = (back_v + routes.core(back_v_sibling)).reshape(rank, 4, rows)
    back_v = back_v[:, 0::2] + routes.across_y(back_v[:, 1::2])
    back_v = back_v[:, 0] + routes.down(back_v[:, 1])
    back = sum_over_tensor(jnp.concatenate((back_q, back_v), axis=0)).astype(BF16)
    grad_down = dot(back, hidden_in, NN).astype(BF16)
    odd = lax.axis_index("seq") % 2 == 1
    of_query, of_value = grad_down[:rank], grad_down[rank:]
    total = add_up(jnp.where(odd, of_value, of_query), swap(jnp.where(odd, of_query, of_value), 1))
    kept, sent = split_for_core(jnp.concatenate((grad_up_q, grad_up_v), axis=1))
    grad_up = sum_over_chips(add_up(kept, swap(sent, 1)), 2)
    total, grad_up = lax.optimization_barrier((add_up(total, swap(total, 2)), grad_up))
    total = sum_over_chips(total, 4)
    grad_up = join_cores(grad_up).astype(F32)
    got = swap(total, 1)
    return (
        attention,
        jnp.where(odd, got, total).astype(F32).T,
        grad_up[:, :-kv_width],
        jnp.where(odd, total, got).astype(F32).T,
        grad_up[:, -kv_width:],
    )


def solution(mesh):
    placed = (
        P("seq", "tensor"),
        P("seq", "tensor"),
        P("seq", "tensor"),
        P("seq", "tensor"),
        P("tensor", None),
        P(None, "tensor"),
        P("tensor", None),
        P(None, "tensor"),
        P("seq", "tensor"),
    )
    return jax.shard_map(
        per_device,
        mesh=mesh,
        in_specs=placed,
        out_specs=(
            P("seq", "tensor"),
            P("tensor", None),
            P(None, "tensor"),
            P("tensor", None),
            P(None, "tensor"),
        ),
        check_vma=False,
    )
```
